512 devices in a mesh: tok: 64 (over y_hi, z, x), head: 8 (over y_lo, core).
Axes of the slice: x: 4, y: 8 (y_hi: 2, y_lo: 4; y = y_hi * 4 + y_lo), z: 8, core: 2. Of those that a mesh axis runs over, the one named last changes fastest.
Arguments:
- text_queries: bfloat16 [256, 8192], P('tok', 'head'), may hold values from -6 to 6
- text_grads: bfloat16 [256, 8192], P('tok', 'head'), may hold values from -6 to 6
- vision_keys: bfloat16 [32768, 1024], P('tok', 'head'), may hold values from -6 to 6
- video_value_rows: bfloat16 [32768, 1024], P('tok', 'head'), may hold values from -6 to 6
- vision: bfloat16 [32768, 4096], P('tok'), may hold values from -16 to 16
- lengths: int32 [8], replicated, may hold values from 16 to 48, as said below
- frame_range: int32 [8, 2], replicated, may hold values from 0 to 256, as said below
Outputs:
- query_grad: bfloat16 [256, 8192], P(None, 'head')
- key_weight_grad: float32 [4096, 1024], P('tok', 'head')
- value_weight_grad: float32 [4096, 1024], P('tok', 'head')
The draws below stay inside these ranges and needn't reach their ends.
Inputs may be any that keep to these rules, and one draw needn't show every extreme that they name: Each segment holds at least one row; the lengths sum to 256. `frame_range`: each segment's range covers 256 // 4 frames or more, first entry below the second.
All inputs are finite; a program needn't handle non-finite values.
Results may differ from the reference program's by a relative error of at most 0.0073.
Values may be sent and summed in bfloat16 or wider, within the bound.
No kernel may reach another device: no remote copies, remote signals or barrier semaphores. Data moves between devices by JAX's collectives and lax.ppermute only.
A program may use at most 64 MiB of HBM per device.

```python
import jax
import jax.numpy as jnp
from jax import lax

QUERY_HEADS = 64
KEY_VALUE_HEADS = 8
HEAD_WIDTH = 128
DW = 4096
TQ = 256
TEXT_SEGMENTS = 8
FRAME_TOK = 128
FRAMES = 256
VIDEO_TOKENS = 32768


def layout(key):
    base_key = jax.random.fold_in(key, 7001)
    base_rows = TQ // TEXT_SEGMENTS
    spread = base_rows // 4
    shifts = jax.random.randint(jax.random.fold_in(base_key, 1), (TEXT_SEGMENTS,), -spread, spread + 1)
    segment_ids = jnp.arange(TEXT_SEGMENTS, dtype=jnp.int32)
    shifts = jnp.where(segment_ids <= 1, spread, shifts)
    shifts = jnp.where(segment_ids == 2, -spread, shifts)
    shifts = jnp.where(segment_ids == TEXT_SEGMENTS - 1, -spread, shifts)
    seg_rows = base_rows + shifts - jnp.roll(shifts, 1)
    fewest = FRAMES // 4
    first_frame = jax.random.randint(jax.random.fold_in(base_key, 2), (TEXT_SEGMENTS,), 0, FRAMES - fewest + 1)
    first_frame = jnp.where(segment_ids == 0, 0, first_frame)
    extension = jax.random.randint(jax.random.fold_in(base_key, 3), (TEXT_SEGMENTS,), 0, FRAMES - fewest - first_frame + 1)
    extension = jnp.where(segment_ids == 1, FRAMES - fewest - first_frame, extension)
    end_frame = first_frame + fewest + extension
    ranges = jnp.stack([first_frame, end_frame], axis=1)
    return (seg_rows.astype(jnp.int32), ranges.astype(jnp.int32))


def paired(key):
    paired_key = jax.random.fold_in(key, 7002)
    query_rows = jnp.clip(1.5 * jax.random.normal(jax.random.fold_in(paired_key, 5), (TQ, QUERY_HEADS * HEAD_WIDTH), jnp.float32), -5.5, 5.5)
    key_row_block = jnp.clip(1.5 * jax.random.normal(jax.random.fold_in(paired_key, 6), (VIDEO_TOKENS, KEY_VALUE_HEADS * HEAD_WIDTH), jnp.float32), -5.5, 5.5)
    return (query_rows, key_row_block)


def draw_lengths(key, part):
    return layout(key)[0]


def draw_frame_range(key, part):
    return layout(key)[1]


def draw_text_queries(key, part):
    return paired(key)[0].astype(jnp.bfloat16)


def draw_vision_keys(key, part):
    return paired(key)[1].astype(jnp.bfloat16)


def spiked(drawn, rng, source, target, parts, factor):
    owner, partner = [(jnp.arange(drawn.shape[dim]) // (drawn.shape[dim] // parts)).reshape([-1 if axis == dim else 1 for axis in range(drawn.ndim)]) for dim in (source, target)]
    chosen = jax.random.permutation(rng, parts)[partner]
    strong = (owner == chosen) | (owner == (partner + parts // 2) % parts)
    return jnp.where(strong, factor * drawn, drawn)


def steps_of(stream_key, dims, pieces, least, high):
    def one(dim, parts):
        heights = jax.random.uniform(jax.random.fold_in(jax.random.fold_in(stream_key, 6), dim), (parts,), jnp.float32, least / len(pieces), high / len(pieces))
        return jnp.repeat(jnp.exp(heights), dims[dim] // parts).reshape((-1,) + (1,) * (len(dims) - dim - 1))

    factor_of = one(*pieces[0])
    for cut in pieces[1:]:
        factor_of = factor_of * one(*cut)
    return factor_of


def noise(key, shape, scale, limit, shards=(), kind=jnp.bfloat16):
    factor_of = steps_of(key, shape, shards, -0.22, 0.18) if shards else 1.0
    drawn = jax.random.normal(key, shape, jnp.float32) * scale * factor_of
    return jnp.minimum(jnp.maximum(drawn, -limit), limit).astype(kind)


def noise_with(key, extent, scale, bound, shards, heavy, held_as=jnp.bfloat16):
    drawn = scale * jax.random.normal(key, extent, jnp.float32)
    if shards:
        drawn = drawn * steps_of(key, extent, shards, -0.22, 0.18)
    return jnp.clip(spiked(drawn, jax.random.fold_in(key, 3), *heavy), -bound, bound).astype(held_as)


def setup_inputs(seed: int = 0) -> dict:
    splits = jax.random.split(jax.random.key(seed), 8)
    return {
        "text_queries": draw_text_queries(jax.random.fold_in(splits[7], 71), 0),
        "text_grads": noise(splits[1], (TQ, QUERY_HEADS * HEAD_WIDTH), 1.0, 6.0, ((0, 64), (1, 8))),
        "vision_keys": draw_vision_keys(jax.random.fold_in(splits[7], 71), 0),
        "video_value_rows": noise(splits[3], (VIDEO_TOKENS, KEY_VALUE_HEADS * HEAD_WIDTH), 1.0, 6.0, ((0, 64), (1, 8))),
        "vision": noise_with(splits[4], (VIDEO_TOKENS, DW), 1.0, 16.0, ((0, 64),), (0, 1, 64, 4.0)),
        "lengths": draw_lengths(jax.random.fold_in(splits[7], 71), 0),
        "frame_range": draw_frame_range(jax.random.fold_in(splits[7], 71), 0),
    }


NEG_FILL = -1e30


def row_bounds(lengths, frame_range):
    row_ids = jnp.arange(TQ, dtype=jnp.int32)
    segment_ends = jnp.cumsum(lengths).astype(jnp.int32)
    segment = jnp.sum((row_ids[:, None] >= segment_ends[None, :]).astype(jnp.int32), axis=1)
    segment_pick = (segment[:, None] == jnp.arange(TEXT_SEGMENTS, dtype=jnp.int32)[None, :]).astype(jnp.int32)
    first_frame = jnp.sum(segment_pick * frame_range[None, :, 0], axis=1)
    end_frame = jnp.sum(segment_pick * frame_range[None, :, 1], axis=1)
    return first_frame, end_frame


def reference(text_queries, text_grads, vision_keys, video_value_rows, vision, lengths, frame_range):
    group_width = QUERY_HEADS // KEY_VALUE_HEADS
    score_scale = HEAD_WIDTH ** -0.5
    first_frame, end_frame = row_bounds(lengths, frame_range)
    frames = jnp.arange(VIDEO_TOKENS, dtype=jnp.int32) // FRAME_TOK
    allowed = (frames[None, :] >= first_frame[:, None]) & (frames[None, :] < end_frame[:, None])

    def head_gradient_list(kv_head):
        k_head = lax.dynamic_slice_in_dim(vision_keys, kv_head * HEAD_WIDTH, HEAD_WIDTH, 1)
        v_head = lax.dynamic_slice_in_dim(video_value_rows, kv_head * HEAD_WIDTH, HEAD_WIDTH, 1)

        def query_head(running, member):
            q_index = kv_head * group_width + member
            q_one = lax.dynamic_slice_in_dim(text_queries, q_index * HEAD_WIDTH, HEAD_WIDTH, 1)
            g_one = lax.dynamic_slice_in_dim(text_grads, q_index * HEAD_WIDTH, HEAD_WIDTH, 1)
            scores = jnp.dot(q_one, k_head.T, preferred_element_type=jnp.float32) * score_scale
            row_top = jnp.max(jnp.where(allowed, scores, NEG_FILL), axis=1, keepdims=True)
            exp_terms = jnp.where(allowed, jnp.exp(scores - row_top), 0.0)
            row_total = jnp.sum(exp_terms, axis=1, keepdims=True)
            attn_probs = exp_terms / row_total
            dprobs = jnp.dot(g_one, v_head.T, preferred_element_type=jnp.float32)
            row_delta = jnp.sum(attn_probs * dprobs, axis=1, keepdims=True)
            dscore = (attn_probs * (dprobs - row_delta)).astype(jnp.bfloat16)
            key_sum = running[0] + jnp.dot(dscore.T, q_one, preferred_element_type=jnp.float32)
            value_sum = running[1] + jnp.dot(attn_probs.astype(jnp.bfloat16).T, g_one, preferred_element_type=jnp.float32)
            dq_part = score_scale * jnp.dot(dscore, k_head, preferred_element_type=jnp.float32)
            return (key_sum, value_sum), dq_part

        zero_acc = jnp.zeros((VIDEO_TOKENS, HEAD_WIDTH), jnp.float32)
        sums, dq_parts = lax.scan(query_head, (zero_acc, zero_acc), jnp.arange(group_width, dtype=jnp.int32))
        return dq_parts, (score_scale * sums[0]).astype(jnp.bfloat16), sums[1].astype(jnp.bfloat16)

    query_gradient_total, key_gradient_total, value_gradient_total = lax.map(head_gradient_list, jnp.arange(KEY_VALUE_HEADS, dtype=jnp.int32))
    query_grad = query_gradient_total.transpose(2, 0, 1, 3).reshape(TQ, QUERY_HEADS * HEAD_WIDTH).astype(jnp.bfloat16)
    key_gradient_flat = key_gradient_total.transpose(1, 0, 2).reshape(VIDEO_TOKENS, KEY_VALUE_HEADS * HEAD_WIDTH)
    value_gradient_flat = value_gradient_total.transpose(1, 0, 2).reshape(VIDEO_TOKENS, KEY_VALUE_HEADS * HEAD_WIDTH)
    key_weight_grad = jnp.dot(vision.T, key_gradient_flat, preferred_element_type=jnp.float32)
    value_weight_grad = jnp.dot(vision.T, value_gradient_flat, preferred_element_type=jnp.float32)
    return query_grad, key_weight_grad, value_weight_grad
```

```python
import jax
import jax.numpy as jnp
from jax import lax
from jax.experimental import pallas as pl
from jax.experimental.pallas import tpu as pltpu
from jax.sharding import Mesh
from jax.sharding import PartitionSpec as P

HEAD_WIDTH = 128
FRAME_DEV = 4
TOK = ("tok_0", "tok_1", "tok_2")
CHUNK = 256
SCALE = HEAD_WIDTH**-0.5
LOG2E = 1.4426950408889634
OFF = 1e30
LOW = -1e29
F32 = jnp.float32
BF16 = jnp.bfloat16
NT = (((1,), (1,)), ((), ()))
NN = (((1,), (0,)), ((), ()))
PARAMS = pltpu.CompilerParams(vmem_limit_bytes=48 * 2**20)


def from_everyone(x, axis):
    peers = lax.axis_size(axis)
    return lax.all_to_all(jnp.broadcast_to(x[None], (peers, *x.shape)), axis, 0, 0, tiled=True)


def dot(a, b, dims):
    return lax.dot_general(a, b, dims, preferred_element_type=F32)


def chunk_of(text_ref, c, which):
    per = CHUNK // text_ref.shape[2]
    return text_ref[c * per : (c + 1) * per, which].reshape(CHUNK, HEAD_WIDTH)


def stats_kernel(text_ref, k_ref, v_ref, off_ref, out_ref):
    chunks = out_ref.shape[0] // 3
    frames = off_ref.shape[1]
    rows = k_ref.shape[0] // frames
    for c in range(chunks):
        scores = dot(k_ref[...], chunk_of(text_ref, c, 0), NT) * (SCALE * LOG2E)
        dprobs = dot(v_ref[...], chunk_of(text_ref, c, 1), NT)
        top = jnp.full((1, CHUNK), LOW, F32)
        for f in range(frames):
            high = jnp.max(scores[f * rows : (f + 1) * rows], axis=0, keepdims=True)
            top = jnp.maximum(top, high - off_ref[c, f : f + 1, :])
        total = jnp.zeros((1, CHUNK), F32)
        weighted = jnp.zeros((1, CHUNK), F32)
        for f in range(frames):
            here = slice(f * rows, (f + 1) * rows)
            terms = jnp.exp2(scores[here] - (top + off_ref[c, f : f + 1, :]))
            total += jnp.sum(terms, axis=0, keepdims=True)
            weighted += jnp.sum(terms * dprobs[here], axis=0, keepdims=True)
        out_ref[c : c + 1, :] = top
        out_ref[chunks + c : chunks + c + 1, :] = total
        out_ref[2 * chunks + c : 2 * chunks + c + 1, :] = weighted


def joined(stats_ref):
    peers, lines = stats_ref.shape[0], stats_ref.shape[1] // 3
    top = stats_ref[0, :lines]
    for k in range(1, peers):
        top = jnp.maximum(top, stats_ref[k, :lines])
    total = jnp.zeros_like(top)
    weighted = jnp.zeros_like(top)
    for k in range(peers):
        factor = jnp.exp2(stats_ref[k, :lines] - top)
        total += stats_ref[k, lines : 2 * lines] * factor
        weighted += stats_ref[k, 2 * lines :] * factor
    return top, total, weighted


def join_kernel(stats_ref, out_ref):
    lines = out_ref.shape[0] // 3
    for k, part in enumerate(joined(stats_ref)):
        out_ref[k * lines : (k + 1) * lines] = part


def grads_kernel(text_ref, k_ref, v_ref, off_ref, stats_ref, kv_ref, dq_ref, p_scr, ds_scr):
    top, total, weighted = joined(stats_ref)
    shift = top + jnp.log2(total)
    delta = weighted / total
    frames = off_ref.shape[1]
    rows = k_ref.shape[0] // frames
    per = CHUNK // dq_ref.shape[1]
    k_all = k_ref[...]
    k_t = k_all.T
    key_sum = jnp.zeros(k_ref.shape, F32)
    value_sum = jnp.zeros(v_ref.shape, F32)
    for c in range(top.shape[0]):
        q_c = chunk_of(text_ref, c, 0)
        g_c = chunk_of(text_ref, c, 1)
        scores = dot(k_all, q_c, NT) * (SCALE * LOG2E)
        dprobs = dot(v_ref[...], g_c, NT)
        for f in range(frames):
            here = slice(f * rows, (f + 1) * rows)
            probs = jnp.exp2(scores[here] - (shift[c : c + 1] + off_ref[c, f : f + 1, :]))
            p_scr[here] = probs.astype(BF16)
            ds_scr[here] = (probs * (dprobs[here] - delta[c : c + 1])).astype(BF16)
        p_c = p_scr[...]
        ds_c = ds_scr[...]
        value_sum += dot(p_c, g_c, NN)
        key_sum += dot(ds_c, q_c, NN)
        dq = (dot(k_t, ds_c, NN) * SCALE).T
        dq_ref[c * per : (c + 1) * per] = dq.reshape(per, dq_ref.shape[1], HEAD_WIDTH)
    kv_ref[:, :HEAD_WIDTH] = (key_sum * SCALE).astype(BF16)
    kv_ref[:, HEAD_WIDTH:] = value_sum.astype(BF16)


def weight_kernel(vision_ref, kv_ref, out_ref):
    out_ref[...] = dot(vision_ref[...], kv_ref[...], NN).astype(BF16)


def offsets(lengths, frame_range, rows, first, frames):
    part_ids = jnp.arange(lengths.shape[0], dtype=jnp.int32)
    ends = jnp.sum(jnp.where(part_ids[None, :] <= part_ids[:, None], lengths[None, :], 0), axis=1)
    segment = jnp.sum((rows[:, None] >= ends[None, :]).astype(jnp.int32), axis=1)
    pick = (segment[:, None] == part_ids[None, :]).astype(jnp.int32)
    begin = jnp.sum(pick * frame_range[None, :, 0], axis=1)
    end = jnp.sum(pick * frame_range[None, :, 1], axis=1)
    at = first + jnp.arange(frames, dtype=jnp.int32)
    allowed = (at[:, None] >= begin[None, :]) & (at[:, None] < end[None, :])
    off = jnp.where(allowed, 0.0, OFF).astype(F32)
    return off.reshape(frames, -1, CHUNK).transpose(1, 0, 2)


def shards(text_queries, text_grads, vision_keys, video_value_rows, vision, lengths, frame_range):
    peers = lax.axis_size(TOK)
    own_rows = text_queries.shape[0]
    members = text_queries.shape[1] // HEAD_WIDTH
    lines = own_rows * members
    kv_rows = vision_keys.shape[0]
    features = vision.shape[1]
    far = lax.axis_size("tok_0") * lax.axis_size("tok_1")
    near = lax.axis_size("tok_2")

    own_text = jnp.stack(
        (text_queries.reshape(lines, HEAD_WIDTH), text_grads.reshape(lines, HEAD_WIDTH))
    )
    text = from_everyone(own_text, TOK)
    text = text.reshape(peers, 2, lines, HEAD_WIDTH)

    row_of = jnp.arange(peers * lines, dtype=jnp.int32) // members
    off = offsets(lengths, frame_range, row_of, lax.axis_index(TOK) * FRAME_DEV, FRAME_DEV)
    vision_t = (
        vision.reshape(kv_rows, far, near, features // peers)
        .transpose(2, 1, 3, 0)
        .reshape(features, kv_rows)
    )

    chunks = peers * lines // CHUNK
    whole = pl.BlockSpec(memory_space=pltpu.VMEM)
    stats = pl.pallas_call(
        stats_kernel,
        out_shape=jax.ShapeDtypeStruct((3 * chunks, CHUNK), F32),
        in_specs=[whole] * 4,
        out_specs=whole,
        compiler_params=PARAMS,
    )(text, vision_keys, video_value_rows, off)

    stats = from_everyone(stats, ("tok_0", "tok_2"))
    stats = pl.pallas_call(
        join_kernel,
        out_shape=jax.ShapeDtypeStruct((3 * chunks, CHUNK), F32),
        in_specs=[whole],
        out_specs=whole,
        compiler_params=PARAMS,
    )(stats.reshape(-1, 3 * chunks, CHUNK))
    stats = from_everyone(stats, "tok_1").reshape(-1, 3 * chunks, CHUNK)

    kv_data, dq = pl.pallas_call(
        grads_kernel,
        out_shape=(
            jax.ShapeDtypeStruct((kv_rows, 2 * HEAD_WIDTH), BF16),
            jax.ShapeDtypeStruct((peers, lines, HEAD_WIDTH), F32),
        ),
        in_specs=[whole] * 5,
        out_specs=(whole, whole),
        scratch_shapes=[
            pltpu.VMEM((kv_rows, CHUNK), BF16),
            pltpu.VMEM((kv_rows, CHUNK), BF16),
        ],
        compiler_params=PARAMS,
    )(text, vision_keys, video_value_rows, off, stats)

    blocks = 8
    part = pl.pallas_call(
        weight_kernel,
        out_shape=jax.ShapeDtypeStruct((features, 2 * HEAD_WIDTH), BF16),
        grid=(blocks,),
        in_specs=[
            pl.BlockSpec((features // blocks, kv_rows), lambda i: (i, 0)),
            pl.BlockSpec((kv_rows, 2 * HEAD_WIDTH), lambda i: (0, 0)),
        ],
        out_specs=pl.BlockSpec((features // blocks, 2 * HEAD_WIDTH), lambda i: (i, 0)),
        compiler_params=PARAMS,
    )(vision_t, kv_data)

    got = lax.all_to_all(
        part.reshape(near, features // near, 2 * HEAD_WIDTH), "tok_2", 0, 0, tiled=True
    )
    part = jnp.sum(got.astype(F32), axis=0).astype(BF16)
    got = lax.all_to_all(
        part.reshape(far, features // peers, 2 * HEAD_WIDTH), ("tok_0", "tok_1"), 0, 0, tiled=True
    )
    weights = jnp.sum(got.astype(F32), axis=0)

    dq = jnp.sum(lax.all_to_all(dq, TOK, 0, 0, tiled=True), axis=0).astype(BF16)
    query_grad = from_everyone(dq.reshape(own_rows, -1), TOK).reshape(peers * own_rows, -1)
    return query_grad, weights[:, :HEAD_WIDTH], weights[:, HEAD_WIDTH:]


def solution(mesh):
    finer = Mesh(
        mesh.devices.reshape(2, 8, 4, mesh.shape["head"]), ("tok_0", "tok_1", "tok_2", "head")
    )
    return jax.shard_map(
        shards,
        mesh=finer,
        in_specs=(
            P(TOK, "head"),
            P(TOK, "head"),
            P(TOK, "head"),
            P(TOK, "head"),
            P(TOK, None),
            P(),
            P(),
        ),
        out_specs=(P(None, "head"), P(TOK, "head"), P(TOK, "head")),
        check_vma=False,
    )
```

```python
import jax
import jax.numpy as jnp
from jax import lax
from jax.experimental import pallas as pl
from jax.experimental.pallas import tpu as pltpu
from jax.sharding import Mesh
from jax.sharding import PartitionSpec as P

HEAD_WIDTH = 128
FRAME_DEV = 4
TOK = ("tok_0", "tok_1", "tok_2")
FAR = ("tok_0", "tok_1")
NEAR = "tok_2"
CHUNK = 256
SCALE = HEAD_WIDTH**-0.5
LOG2E = 1.4426950408889634
OFF = 1e30
LOW = -1e29
F32 = jnp.float32
BF16 = jnp.bfloat16
NT = (((1,), (1,)), ((), ()))
NN = (((1,), (0,)), ((), ()))
PARAMS = pltpu.CompilerParams(vmem_limit_bytes=32 * 2**20)
WHOLE = pl.BlockSpec(memory_space=pltpu.VMEM)
SCALARS = pl.BlockSpec(memory_space=pltpu.SMEM)


def from_everyone(x, axis):
    peers = lax.axis_size(axis)
    return lax.all_to_all(jnp.broadcast_to(x[None], (peers, *x.shape)), axis, 0, 0, tiled=True)


def shifted(x, axis, step):
    peers = lax.axis_size(axis)
    return lax.ppermute(x, axis, [(i, (i + step) % peers) for i in range(peers)])


def dot(a, b, dims):
    return lax.dot_general(a, b, dims, preferred_element_type=F32)


def chunk_of(text_ref, c, which):
    per = CHUNK // text_ref.shape[2]
    return text_ref[c * per : (c + 1) * per, which].reshape(CHUNK, HEAD_WIDTH)


def frame_slices(off_ref, c, rows, frames):
    for f in range(frames):
        yield slice(f * rows, (f + 1) * rows), off_ref[c, f : f + 1, :]


def join(parts):
    top = parts[0][0]
    for part in parts[1:]:
        top = jnp.maximum(top, part[0])
    total = jnp.zeros_like(top)
    weighted = jnp.zeros_like(top)
    for part in parts:
        factor = jnp.exp2(part[0] - top)
        total += part[1] * factor
        weighted += part[2] * factor
    return top, total, weighted


def stats_kernel(text_ref, off_ref, *refs):
    kv_refs, out_ref = refs[:-1], refs[-1]
    chunks = out_ref.shape[0] // 3
    for c in range(chunks):
        q_c, g_c = chunk_of(text_ref, c, 0), chunk_of(text_ref, c, 1)
        parts = []
        for p, kv_ref in enumerate(kv_refs):
            rows = kv_ref.shape[1] // FRAME_DEV
            scores = dot(kv_ref[0], q_c, NT) * (SCALE * LOG2E)
            dprobs = dot(kv_ref[1], g_c, NT)
            offs = off_ref.at[:, p * FRAME_DEV : (p + 1) * FRAME_DEV]
            top = jnp.full((1, CHUNK), LOW, F32)
            for here, off in frame_slices(offs, c, rows, FRAME_DEV):
                top = jnp.maximum(top, jnp.max(scores[here], axis=0, keepdims=True) - off)
            total = jnp.zeros((1, CHUNK), F32)
            weighted = jnp.zeros((1, CHUNK), F32)
            for here, off in frame_slices(offs, c, rows, FRAME_DEV):
                terms = jnp.exp2(scores[here] - (top + off))
                total += jnp.sum(terms, axis=0, keepdims=True)
                weighted += jnp.sum(terms * dprobs[here], axis=0, keepdims=True)
            parts.append((top, total, weighted))
        for k, part in enumerate(join(parts)):
            out_ref[k * chunks + c : k * chunks + c + 1, :] = part


def join_kernel(stats_ref, out_ref):
    lines = stats_ref.shape[1] // 3
    parts = [
        [stats_ref[k, j * lines : (j + 1) * lines] for j in range(3)]
        for k in range(stats_ref.shape[0])
    ]
    top, total, weighted = join(parts)
    out_ref[:lines] = top + jnp.log2(total)
    out_ref[lines:] = weighted / total


def query_kernel(text_ref, off_ref, norm_ref, *refs):
    kv_refs, dq_ref, ds_scr = refs[:-2], refs[-2], refs[-1]
    chunks = norm_ref.shape[0] // 2
    per = CHUNK // dq_ref.shape[1]
    for c in range(chunks):
        q_c, g_c = chunk_of(text_ref, c, 0), chunk_of(text_ref, c, 1)
        shift = norm_ref[c : c + 1, :]
        delta = norm_ref[chunks + c : chunks + c + 1, :]
        dq = jnp.zeros((HEAD_WIDTH, CHUNK), F32)
        for p, kv_ref in enumerate(kv_refs):
            rows = kv_ref.shape[1] // FRAME_DEV
            scores = dot(kv_ref[0], q_c, NT) * (SCALE * LOG2E)
            dprobs = dot(kv_ref[1], g_c, NT)
            offs = off_ref.at[:, p * FRAME_DEV : (p + 1) * FRAME_DEV]
            for here, off in frame_slices(offs, c, rows, FRAME_DEV):
                probs = jnp.exp2(scores[here] - (shift + off))
                ds_scr[here] = (probs * (dprobs[here] - delta)).astype(BF16)
            dq += dot(kv_ref[0].T, ds_scr[...], NN)
        dq_ref[c * per : (c + 1) * per] = (dq * SCALE).T.reshape(per, dq_ref.shape[1], HEAD_WIDTH)


def token_kernel(near_ref, kv_ref, off_ref, norm_ref, far_vision_ref, *refs):
    pieces = off_ref.shape[0]
    text_refs, out_refs = refs[:pieces], refs[pieces : 2 * pieces]
    p_scr, ds_scr, kv_scr, vision_ref, vision_sem = refs[2 * pieces :]
    vision_copy = pltpu.make_async_copy(far_vision_ref, vision_ref, vision_sem)
    vision_copy.start()
    chunks = norm_ref.shape[1] // 2
    rows = kv_ref.shape[1] // FRAME_DEV
    key_sum = jnp.zeros(kv_ref.shape[1:], F32)
    value_sum = jnp.zeros(kv_ref.shape[1:], F32)
    for p, text_ref in enumerate(text_refs):
        norm = norm_ref[(near_ref[0] + (pieces - p)) % pieces]
        for c in range(chunks):
            q_c, g_c = chunk_of(text_ref, c, 0), chunk_of(text_ref, c, 1)
            shift, delta = norm[c : c + 1], norm[chunks + c : chunks + c + 1]
            scores = dot(kv_ref[0], q_c, NT) * (SCALE * LOG2E)
            dprobs = dot(kv_ref[1], g_c, NT)
            for here, off in frame_slices(off_ref.at[p], c, rows, FRAME_DEV):
                probs = jnp.exp2(scores[here] - (shift + off))
                p_scr[here] = probs.astype(BF16)
                ds_scr[here] = (probs * (dprobs[here] - delta)).astype(BF16)
            value_sum += dot(p_scr[...], g_c, NN)
            key_sum += dot(ds_scr[...], q_c, NN)
    kv_scr[:, :HEAD_WIDTH] = (key_sum * SCALE).astype(BF16)
    kv_scr[:, HEAD_WIDTH:] = value_sum.astype(BF16)
    vision_copy.wait()
    size = 512
    for p, out_ref in enumerate(out_refs):
        for at in range(0, out_ref.shape[0], size):
            block = vision_ref[p, at : at + size]
            out_ref[at : at + size] = dot(block, kv_scr[...], NN).astype(BF16)


def turn_kernel(near_ref, vision_ref, out_ref):
    pieces, _, size, _ = out_ref.shape
    turned = vision_ref[...].T
    for p in range(pieces):
        at = (p + pieces - near_ref[0]) % pieces
        out_ref[at, 0] = turned[p * size : (p + 1) * size]


def bases_from(at, peers):
    return [lax.rem(at + peers - k, jnp.int32(peers)) for k in range(peers)]


def row_bounds(lengths, frame_range, rows):
    part_ids = jnp.arange(lengths.shape[0], dtype=jnp.int32)
    ends = jnp.sum(jnp.where(part_ids[None, :] <= part_ids[:, None], lengths[None, :], 0), axis=1)
    segment = jnp.sum((rows[:, None] >= ends[None, :]).astype(jnp.int32), axis=1)
    pick = (segment[:, None] == part_ids[None, :]).astype(jnp.int32)
    begin = jnp.sum(pick * frame_range[None, :, 0], axis=1)
    end = jnp.sum(pick * frame_range[None, :, 1], axis=1)
    return begin, end


def offsets(begin, end, at):
    allowed = (at[:, None] >= begin[None, :]) & (at[:, None] < end[None, :])
    off = jnp.where(allowed, 0.0, OFF).astype(F32)
    return off.reshape(at.shape[0], -1, CHUNK).transpose(1, 0, 2)


def shards(text_queries, text_grads, vision_keys, video_value_rows, vision, lengths, frame_range):
    far, near = lax.axis_size(FAR), lax.axis_size(NEAR)
    my_far, my_near = lax.axis_index(FAR), lax.axis_index(NEAR)
    peers = far * near
    own_rows = text_queries.shape[0]
    members = text_queries.shape[1] // HEAD_WIDTH
    lines = own_rows * members
    kv_rows = vision_keys.shape[0]
    features = vision.shape[1]
    near_id = my_near.reshape(1).astype(jnp.int32)

    own_text = jnp.stack(
        (text_queries.reshape(lines, HEAD_WIDTH), text_grads.reshape(lines, HEAD_WIDTH))
    )
    text = from_everyone(own_text, FAR).reshape(far, 2, lines, HEAD_WIDTH)
    own_kv = jnp.stack((vision_keys, video_value_rows))
    all_kv = [own_kv] + [shifted(own_kv, NEAR, k) for k in range(1, near)]
    all_text = [text] + [shifted(text, NEAR, k) for k in range(1, near)]

    line_ids = jnp.arange(far * lines, dtype=jnp.int32)
    sources = jnp.stack(bases_from(my_near, near))
    row_of = (
        (line_ids // lines)[None, :] * (near * own_rows)
        + sources[:, None] * own_rows
        + (line_ids % lines // members)[None, :]
    )
    begin, end = row_bounds(lengths, frame_range, row_of.reshape(-1))
    steps = jnp.arange(FRAME_DEV, dtype=jnp.int32)
    first = (my_far * near + sources) * FRAME_DEV
    group_frames = (first[:, None] + steps[None, :]).reshape(-1)
    own_off = offsets(begin[: far * lines], end[: far * lines], group_frames)
    all_off = offsets(begin, end, first[0] + steps)
    chunks = far * lines // CHUNK
    all_off = all_off.reshape(near, chunks, FRAME_DEV, CHUNK)

    part = features // peers
    turned = pl.pallas_call(
        turn_kernel,
        out_shape=jax.ShapeDtypeStruct((near, far, part, kv_rows), BF16),
        grid=(far,),
        in_specs=[SCALARS, pl.BlockSpec((kv_rows, near * part), lambda i: (0, i))],
        out_specs=pl.BlockSpec((near, 1, part, kv_rows), lambda i: (0, i, 0, 0)),
        compiler_params=PARAMS,
    )(near_id, vision)
    turned = turned.reshape(near, far * part, kv_rows)
    text, turned = lax.optimization_barrier((text, turned))

    stats = pl.pallas_call(
        stats_kernel,
        out_shape=jax.ShapeDtypeStruct((3 * chunks, CHUNK), F32),
        in_specs=[WHOLE] * (2 + near),
        out_specs=WHOLE,
        compiler_params=PARAMS,
    )(text, own_off, *all_kv)
    stats = from_everyone(stats, FAR).reshape(far, 3 * chunks, CHUNK)
    norm = pl.pallas_call(
        join_kernel,
        out_shape=jax.ShapeDtypeStruct((2 * chunks, CHUNK), F32),
        in_specs=[WHOLE],
        out_specs=WHOLE,
        compiler_params=PARAMS,
    )(stats)
    all_norm = from_everyone(norm, NEAR).reshape(near, 2 * chunks, CHUNK)

    dq = pl.pallas_call(
        query_kernel,
        out_shape=jax.ShapeDtypeStruct((far, lines, HEAD_WIDTH), F32),
        in_specs=[WHOLE] * (3 + near),
        out_specs=WHOLE,
        scratch_shapes=[pltpu.VMEM((kv_rows, CHUNK), BF16)],
        compiler_params=PARAMS,
    )(text, own_off, norm, *all_kv)

    sums = pl.pallas_call(
        token_kernel,
        out_shape=[jax.ShapeDtypeStruct((far * part, 2 * HEAD_WIDTH), BF16)] * near,
        in_specs=[SCALARS] + [WHOLE] * 3 + [pl.BlockSpec(memory_space=pl.ANY)] + [WHOLE] * near,
        out_specs=[WHOLE] * near,
        scratch_shapes=[
            pltpu.VMEM((kv_rows, CHUNK), BF16),
            pltpu.VMEM((kv_rows, CHUNK), BF16),
            pltpu.VMEM((kv_rows, 2 * HEAD_WIDTH), BF16),
            pltpu.VMEM((near, far * part, kv_rows), BF16),
            pltpu.SemaphoreType.DMA,
        ],
        compiler_params=PARAMS,
    )(near_id, own_kv, all_off, all_norm, turned, *all_text)

    sums, dq = lax.optimization_barrier((sums, dq))
    got = [sums[0]] + [shifted(sums[k], NEAR, k) for k in range(1, near)]

    dq = jnp.sum(lax.all_to_all(dq, FAR, 0, 0, tiled=True), axis=0).astype(BF16)
    dq = from_everyone(dq.reshape(own_rows, -1), FAR).reshape(far, own_rows, -1)

    weights = sum(one.astype(F32) for one in got).astype(BF16)
    weights, dq = lax.optimization_barrier((weights, dq))
    weights = lax.all_to_all(
        weights.reshape(far, part, 2 * HEAD_WIDTH), FAR, 0, 0, tiled=True
    )
    all_dq = [dq] + [shifted(dq, NEAR, k) for k in range(1, near)]
    query_grad = jnp.stack([lax.select_n(base, *all_dq) for base in bases_from(my_near, near)], 1)
    query_grad = query_grad.reshape(peers * own_rows, -1)
    weights = jnp.sum(weights.astype(F32), axis=0)
    return query_grad, weights[:, :HEAD_WIDTH], weights[:, HEAD_WIDTH:]


def solution(mesh):
    finer = Mesh(
        mesh.devices.reshape(2, 8, 4, mesh.shape["head"]), ("tok_0", "tok_1", "tok_2", "head")
    )
    return jax.shard_map(
        shards,
        mesh=finer,
        in_specs=(
            P(TOK, "head"),
            P(TOK, "head"),
            P(TOK, "head"),
            P(TOK, "head"),
            P(TOK, None),
            P(),
            P(),
        ),
        out_specs=(P(None, "head"), P(TOK, "head"), P(TOK, "head")),
        check_vma=False,
    )
```

```python
import jax
import jax.numpy as jnp
from jax import lax
from jax.experimental import pallas as pl
from jax.experimental.pallas import tpu as pltpu
from jax.sharding import Mesh
from jax.sharding import PartitionSpec as P

HEAD_WIDTH = 128
FRAME_DEV = 4
TOK = ("tok_0", "tok_1", "tok_2")
FAR = ("tok_0", "tok_1")
NEAR = "tok_2"
CHUNK = 256
SCALE = HEAD_WIDTH**-0.5
LOG2E = 1.4426950408889634
OFF = 1e30
LOW = -1e29
F32 = jnp.float32
BF16 = jnp.bfloat16
NT = (((1,), (1,)), ((), ()))
NN = (((1,), (0,)), ((), ()))
PARAMS = pltpu.CompilerParams(vmem_limit_bytes=32 * 2**20)
LARGE = pltpu.CompilerParams(vmem_limit_bytes=52 * 2**20)
LARGER = pltpu.CompilerParams(vmem_limit_bytes=58 * 2**20)
HEAVY = pl.CostEstimate(flops=10**11, bytes_accessed=2**20, transcendentals=0)
WHOLE = pl.BlockSpec(memory_space=pltpu.VMEM)
SCALARS = pl.BlockSpec(memory_space=pltpu.SMEM)


def from_everyone(x, axis):
    peers = lax.axis_size(axis)
    return lax.all_to_all(jnp.broadcast_to(x[None], (peers, *x.shape)), axis, 0, 0, tiled=True)


def shifted(x, axis, step):
    peers = lax.axis_size(axis)
    return lax.ppermute(x, axis, [(i, (i + step) % peers) for i in range(peers)])


def dot(a, b, dims):
    return lax.dot_general(a, b, dims, preferred_element_type=F32)


def chunk_of(text_ref, c, which):
    per = CHUNK // text_ref.shape[2]
    return text_ref[c * per : (c + 1) * per, which].reshape(CHUNK, HEAD_WIDTH)


def frame_slices(off_ref, c, rows, frames):
    for f in range(frames):
        yield slice(f * rows, (f + 1) * rows), off_ref[c, f : f + 1, :]


def join(parts):
    top = parts[0][0]
    for part in parts[1:]:
        top = jnp.maximum(top, part[0])
    total = jnp.zeros_like(top)
    weighted = jnp.zeros_like(top)
    for part in parts:
        factor = jnp.exp2(part[0] - top)
        total += part[1] * factor
        weighted += part[2] * factor
    return top, total, weighted


def piece_stats(q_c, g_c, kv_ref, off_ref, c):
    rows = kv_ref.shape[1] // FRAME_DEV
    scores = dot(kv_ref[0], q_c, NT) * (SCALE * LOG2E)
    dprobs = dot(kv_ref[1], g_c, NT)
    top = jnp.full((1, CHUNK), LOW, F32)
    for here, off in frame_slices(off_ref, c, rows, FRAME_DEV):
        top = jnp.maximum(top, jnp.max(scores[here], axis=0, keepdims=True) - off)
    total = jnp.zeros((1, CHUNK), F32)
    weighted = jnp.zeros((1, CHUNK), F32)
    for here, off in frame_slices(off_ref, c, rows, FRAME_DEV):
        terms = jnp.exp2(scores[here] - (top + off))
        total += jnp.sum(terms, axis=0, keepdims=True)
        weighted += jnp.sum(terms * dprobs[here], axis=0, keepdims=True)
    return top, total, weighted


def stats_kernel(text_ref, off_ref, *refs):
    kv_refs, all_ref, stats_scr = refs[:-2], refs[-2], refs[-1]
    chunks = stats_scr.shape[0] // 3
    for c in range(chunks):
        q_c, g_c = chunk_of(text_ref, c, 0), chunk_of(text_ref, c, 1)
        parts = []
        for p, kv_ref in enumerate(kv_refs):
            offs = off_ref.at[:, p * FRAME_DEV : (p + 1) * FRAME_DEV]
            parts.append(piece_stats(q_c, g_c, kv_ref, offs, c))
        for k, part in enumerate(join(parts)):
            stats_scr[k * chunks + c : k * chunks + c + 1, :] = part
    stats = stats_scr[...]
    for k in range(all_ref.shape[0]):
        all_ref[k] = stats


def join_kernel(stats_ref, out_ref):
    lines = stats_ref.shape[2] // 3
    for p in range(out_ref.shape[0]):
        parts = [
            [stats_ref[k, p, j * lines : (j + 1) * lines] for j in range(3)]
            for k in range(stats_ref.shape[0])
        ]
        top, total, weighted = join(parts)
        out_ref[p, :lines] = top + jnp.log2(total)
        out_ref[p, lines:] = weighted / total


def query_kernel(near_ref, text_ref, off_ref, all_norm_ref, *refs):
    kv_refs, dq_ref, ds_scr = refs[:-2], refs[-2], refs[-1]
    norm_ref = all_norm_ref.at[near_ref[0]]
    chunks = norm_ref.shape[0] // 2
    per = CHUNK // dq_ref.shape[1]
    for c in range(chunks):
        q_c, g_c = chunk_of(text_ref, c, 0), chunk_of(text_ref, c, 1)
        shift = norm_ref[c : c + 1, :]
        delta = norm_ref[chunks + c : chunks + c + 1, :]
        dq = jnp.zeros((HEAD_WIDTH, CHUNK), F32)
        for p, kv_ref in enumerate(kv_refs):
            rows = kv_ref.shape[1] // FRAME_DEV
            scores = dot(kv_ref[0], q_c, NT) * (SCALE * LOG2E)
            dprobs = dot(kv_ref[1], g_c, NT)
            offs = off_ref.at[:, p * FRAME_DEV : (p + 1) * FRAME_DEV]
            for here, off in frame_slices(offs, c, rows, FRAME_DEV):
                probs = jnp.exp2(scores[here] - (shift + off))
                ds_scr[here] = (probs * (dprobs[here] - delta)).astype(BF16)
            dq += dot(kv_ref[0].T, ds_scr[...], NN)
        dq_ref[c * per : (c + 1) * per] = (dq * SCALE).T.reshape(per, dq_ref.shape[1], HEAD_WIDTH)


def token_kernel(near_ref, kv_ref, off_ref, norm_ref, far_vision_ref, *refs):
    pieces = off_ref.shape[0]
    text_refs, out_refs = refs[:pieces], refs[pieces : 2 * pieces]
    p_scr, ds_scr, kv_scr, vision_ref, vision_sem = refs[2 * pieces :]
    vision_copy = pltpu.make_async_copy(far_vision_ref, vision_ref, vision_sem)
    vision_copy.start()
    chunks = norm_ref.shape[1] // 2
    rows = kv_ref.shape[1] // FRAME_DEV
    key_sum = jnp.zeros(kv_ref.shape[1:], F32)
    value_sum = jnp.zeros(kv_ref.shape[1:], F32)
    for p, text_ref in enumerate(text_refs):
        norm = norm_ref[(near_ref[0] + (pieces - p)) % pieces]
        for c in range(chunks):
            q_c, g_c = chunk_of(text_ref, c, 0), chunk_of(text_ref, c, 1)
            shift, delta = norm[c : c + 1], norm[chunks + c : chunks + c + 1]
            scores = dot(kv_ref[0], q_c, NT) * (SCALE * LOG2E)
            dprobs = dot(kv_ref[1], g_c, NT)
            for here, off in frame_slices(off_ref.at[p], c, rows, FRAME_DEV):
                probs = jnp.exp2(scores[here] - (shift + off))
                p_scr[here] = probs.astype(BF16)
                ds_scr[here] = (probs * (dprobs[here] - delta)).astype(BF16)
            value_sum += dot(p_scr[...], g_c, NN)
            key_sum += dot(ds_scr[...], q_c, NN)
    kv_scr[:, :HEAD_WIDTH] = (key_sum * SCALE).astype(BF16)
    kv_scr[:, HEAD_WIDTH:] = value_sum.astype(BF16)
    vision_copy.wait()
    size = 512
    for p, out_ref in enumerate(out_refs):
        for at in range(0, out_ref.shape[0], size):
            block = vision_ref[p, at : at + size]
            out_ref[at : at + size] = dot(block, kv_scr[...], NN).astype(BF16)


def sum_kernel(parts_ref, out_ref):
    out_ref[...] = jnp.sum(parts_ref[...], axis=0).astype(BF16)


def turn_kernel(near_ref, vision_ref, out_ref):
    pieces, _, size, _ = out_ref.shape
    turned = vision_ref[...].T
    for p in range(pieces):
        at = (p + pieces - near_ref[0]) % pieces
        out_ref[at, 0] = turned[p * size : (p + 1) * size]


def bases_from(at, peers):
    return [lax.rem(at + peers - k, jnp.int32(peers)) for k in range(peers)]


def row_bounds(lengths, frame_range, rows):
    part_ids = jnp.arange(lengths.shape[0], dtype=jnp.int32)
    ends = jnp.sum(jnp.where(part_ids[None, :] <= part_ids[:, None], lengths[None, :], 0), axis=1)
    segment = jnp.sum((rows[:, None] >= ends[None, :]).astype(jnp.int32), axis=1)
    pick = (segment[:, None] == part_ids[None, :]).astype(jnp.int32)
    begin = jnp.sum(pick * frame_range[None, :, 0], axis=1)
    end = jnp.sum(pick * frame_range[None, :, 1], axis=1)
    return begin, end


def offsets(begin, end, at):
    allowed = (at[:, None] >= begin[None, :]) & (at[:, None] < end[None, :])
    off = jnp.where(allowed, 0.0, OFF).astype(F32)
    return off.reshape(at.shape[0], -1, CHUNK).transpose(1, 0, 2)


def shards(text_queries, text_grads, vision_keys, video_value_rows, vision, lengths, frame_range):
    far, near = lax.axis_size(FAR), lax.axis_size(NEAR)
    my_far, my_near = lax.axis_index(FAR), lax.axis_index(NEAR)
    peers = far * near
    own_rows = text_queries.shape[0]
    members = text_queries.shape[1] // HEAD_WIDTH
    lines = own_rows * members
    kv_rows = vision_keys.shape[0]
    features = vision.shape[1]
    near_id = my_near.reshape(1).astype(jnp.int32)

    own_text = jnp.stack(
        (text_queries.reshape(lines, HEAD_WIDTH), text_grads.reshape(lines, HEAD_WIDTH))
    )
    own_text = jnp.broadcast_to(own_text[None], (far, *own_text.shape))
    own_text, vision_keys, video_value_rows = lax.optimization_barrier(
        (own_text, vision_keys, video_value_rows)
    )
    text = lax.all_to_all(own_text, FAR, 0, 0, tiled=True)
    own_kv = jnp.stack((vision_keys, video_value_rows))
    all_kv = [own_kv] + [shifted(own_kv, NEAR, k) for k in range(1, near)]
    all_text = [text] + [shifted(text, NEAR, k) for k in range(1, near)]

    line_ids = jnp.arange(far * lines, dtype=jnp.int32)
    sources = jnp.stack(bases_from(my_near, near))
    row_of = (
        (line_ids // lines)[None, :] * (near * own_rows)
        + sources[:, None] * own_rows
        + (line_ids % lines // members)[None, :]
    )
    begin, end = row_bounds(lengths, frame_range, row_of.reshape(-1))
    steps = jnp.arange(FRAME_DEV, dtype=jnp.int32)
    first = (my_far * near + sources) * FRAME_DEV
    group_frames = (first[:, None] + steps[None, :]).reshape(-1)
    own_off = offsets(begin[: far * lines], end[: far * lines], group_frames)
    all_off = offsets(begin, end, first[0] + steps)
    chunks = far * lines // CHUNK
    all_off = all_off.reshape(near, chunks, FRAME_DEV, CHUNK)

    part = features // peers
    turned = pl.pallas_call(
        turn_kernel,
        out_shape=jax.ShapeDtypeStruct((near, far, part, kv_rows), BF16),
        grid=(far,),
        in_specs=[SCALARS, pl.BlockSpec((kv_rows, near * part), lambda i: (0, i))],
        out_specs=pl.BlockSpec((near, 1, part, kv_rows), lambda i: (0, i, 0, 0)),
        compiler_params=LARGER,
    )(near_id, vision)
    turned = turned.reshape(near, far * part, kv_rows)
    text, turned = lax.optimization_barrier((text, turned))

    stats = pl.pallas_call(
        stats_kernel,
        out_shape=jax.ShapeDtypeStruct((peers, 3 * chunks, CHUNK), F32),
        in_specs=[WHOLE] * (2 + near),
        out_specs=WHOLE,
        scratch_shapes=[pltpu.VMEM((3 * chunks, CHUNK), F32)],
        compiler_params=PARAMS,
    )(text, own_off, *all_kv)
    stats = lax.all_to_all(stats, TOK, 0, 0, tiled=True)
    all_norm = pl.pallas_call(
        join_kernel,
        out_shape=jax.ShapeDtypeStruct((near, 2 * chunks, CHUNK), F32),
        in_specs=[WHOLE],
        out_specs=WHOLE,
        compiler_params=PARAMS,
    )(stats.reshape(far, near, 3 * chunks, CHUNK))

    dq = pl.pallas_call(
        query_kernel,
        out_shape=jax.ShapeDtypeStruct((far, lines, HEAD_WIDTH), F32),
        in_specs=[SCALARS] + [WHOLE] * (3 + near),
        out_specs=WHOLE,
        scratch_shapes=[pltpu.VMEM((kv_rows, CHUNK), BF16)],
        compiler_params=PARAMS,
    )(near_id, text, own_off, all_norm, *all_kv)
    dq = lax.all_to_all(dq, FAR, 0, 0, tiled=True)

    sums = pl.pallas_call(
        token_kernel,
        out_shape=[jax.ShapeDtypeStruct((far * part, 2 * HEAD_WIDTH), BF16)] * near,
        in_specs=[SCALARS] + [WHOLE] * 3 + [pl.BlockSpec(memory_space=pltpu.HBM)] + [WHOLE] * near,
        out_specs=[WHOLE] * near,
        scratch_shapes=[
            pltpu.VMEM((kv_rows, CHUNK), BF16),
            pltpu.VMEM((kv_rows, CHUNK), BF16),
            pltpu.VMEM((kv_rows, 2 * HEAD_WIDTH), BF16),
            pltpu.VMEM((near, far * part, kv_rows), BF16),
            pltpu.SemaphoreType.DMA,
        ],
        compiler_params=LARGE,
        cost_estimate=HEAVY,
    )(near_id, own_kv, all_off, all_norm, turned, *all_text)

    got = [sums[0]] + [shifted(sums[k], NEAR, k) for k in range(1, near)]

    dq = pl.pallas_call(
        sum_kernel,
        out_shape=jax.ShapeDtypeStruct((lines, HEAD_WIDTH), BF16),
        in_specs=[WHOLE],
        out_specs=WHOLE,
        compiler_params=PARAMS,
        cost_estimate=HEAVY,
    )(dq)
    dq = from_everyone(dq.reshape(own_rows, -1), FAR).reshape(far, own_rows, -1)

    weights = sum(one.astype(F32) for one in got).astype(BF16)
    weights, dq = lax.optimization_barrier((weights, dq))
    weights = lax.all_to_all(
        weights.reshape(far, part, 2 * HEAD_WIDTH), FAR, 0, 0, tiled=True
    )
    all_dq = [dq] + [shifted(dq, NEAR, k) for k in range(1, near)]
    query_grad = jnp.stack([lax.select_n(base, *all_dq) for base in bases_from(my_near, near)], 1)
    query_grad = query_grad.reshape(peers * own_rows, -1)
    weights = jnp.sum(weights.astype(F32), axis=0)
    return query_grad, weights[:, :HEAD_WIDTH], weights[:, HEAD_WIDTH:]


def solution(mesh):
    finer = Mesh(
        mesh.devices.reshape(2, 8, 4, mesh.shape["head"]), ("tok_0", "tok_1", "tok_2", "head")
    )
    return jax.shard_map(
        shards,
        mesh=finer,
        in_specs=(
            P(TOK, "head"),
            P(TOK, "head"),
            P(TOK, "head"),
            P(TOK, "head"),
            P(TOK, None),
            P(),
            P(),
        ),
        out_specs=(P(None, "head"), P(TOK, "head"), P(TOK, "head")),
        check_vma=False,
    )
```

```python
import jax
import jax.numpy as jnp
from jax import lax
from jax.experimental import pallas as pl
from jax.experimental.pallas import tpu as pltpu
from jax.sharding import Mesh
from jax.sharding import PartitionSpec as P

HEAD_WIDTH = 128
FRAME_DEV = 4
TOK = ("tok_0", "tok_1", "tok_2")
FAR = ("tok_0", "tok_1")
NEAR = "tok_2"
CHUNK = 256
PART = 64
STATS_LINES = 12
SCALE = HEAD_WIDTH**-0.5
LOG2E = 1.4426950408889634
OFF = 1e30
LOW = -1e29
F32 = jnp.float32
BF16 = jnp.bfloat16
NT = (((1,), (1,)), ((), ()))
NN = (((1,), (0,)), ((), ()))
PARAMS = pltpu.CompilerParams(vmem_limit_bytes=32 * 2**20)
LARGE = pltpu.CompilerParams(vmem_limit_bytes=52 * 2**20)
HEAVY = pl.CostEstimate(flops=10**11, bytes_accessed=2**20, transcendentals=0)
WHOLE = pl.BlockSpec(memory_space=pltpu.VMEM)
SCALARS = pl.BlockSpec(memory_space=pltpu.SMEM)


def from_everyone(x, axis):
    peers = lax.axis_size(axis)
    return lax.all_to_all(jnp.broadcast_to(x[None], (peers, *x.shape)), axis, 0, 0, tiled=True)


def shifted(x, axis, step):
    peers = lax.axis_size(axis)
    return lax.ppermute(x, axis, [(i, (i + step) % peers) for i in range(peers)])


def dot(a, b, dims):
    return lax.dot_general(a, b, dims, preferred_element_type=F32)


def chunk_of(text_ref, c, which):
    per = CHUNK // text_ref.shape[2]
    return text_ref[c * per : (c + 1) * per, which].reshape(CHUNK, HEAD_WIDTH)


def row_bounds(place_ref, lengths_ref, range_ref, near_at, c):
    near, own_rows, lines = place_ref[1], place_ref[2], place_ref[3]
    line = lax.broadcasted_iota(jnp.int32, (1, CHUNK), 1) + c * CHUNK
    row = (lax.div(line, lines) * near + near_at) * own_rows + lax.rem(line, own_rows)
    begin = jnp.zeros((1, CHUNK), jnp.int32)
    end = jnp.zeros((1, CHUNK), jnp.int32)
    at = jnp.int32(0)
    for k in range(lengths_ref.shape[0]):
        stop = at + lengths_ref[k]
        inside = (row >= at) & (row < stop)
        begin = jnp.where(inside, range_ref[k, 0], begin)
        end = jnp.where(inside, range_ref[k, 1], end)
        at = stop
    return begin, end


def frame_slices(bounds, first, rows):
    begin, end = bounds
    for f in range(FRAME_DEV):
        allowed = (begin <= first + f) & (end > first + f)
        off = jnp.where(allowed, 0.0, OFF).astype(F32)
        yield slice(f * rows, (f + 1) * rows), off


def source(near_at, piece, near):
    return lax.rem(near_at + (near - piece), jnp.int32(near))


def join(parts):
    top = parts[0][0]
    for part in parts[1:]:
        top = jnp.maximum(top, part[0])
    total = jnp.zeros_like(top)
    weighted = jnp.zeros_like(top)
    for part in parts:
        factor = jnp.exp2(part[0] - top)
        total += part[1] * factor
        weighted += part[2] * factor
    return top, total, weighted


def piece_stats(q_c, g_c, kv_ref, bounds, first):
    rows = kv_ref.shape[1] // FRAME_DEV
    offs = list(frame_slices(bounds, first, rows))
    scores = dot(kv_ref[0], q_c, NT) * (SCALE * LOG2E)
    dprobs = dot(kv_ref[1], g_c, NT)
    top = jnp.full((1, CHUNK), LOW, F32)
    for here, off in offs:
        top = jnp.maximum(top, jnp.max(scores[here], axis=0, keepdims=True) - off)
    total = jnp.zeros((1, CHUNK), F32)
    weighted = jnp.zeros((1, CHUNK), F32)
    for here, off in offs:
        terms = jnp.exp2(scores[here] - (top + off))
        total += jnp.sum(terms, axis=0, keepdims=True)
        weighted += jnp.sum(terms * dprobs[here], axis=0, keepdims=True)
    return top, total, weighted


def prepare_kernel(q_ref, g_ref, text_ref):
    members = q_ref.shape[1] // HEAD_WIDTH
    for which, ref in enumerate((q_ref, g_ref)):
        rows = ref[...].astype(F32)
        lines = jnp.concatenate(
            [rows[:, m * HEAD_WIDTH : (m + 1) * HEAD_WIDTH] for m in range(members)], axis=0
        ).astype(BF16)
        for k in range(text_ref.shape[0]):
            text_ref[k, which] = lines


def mask_kernel(place_ref, lengths_ref, range_ref, out_ref):
    pieces, chunks = out_ref.shape[:2]
    first = (place_ref[4] + place_ref[0]) * FRAME_DEV
    for p in range(pieces):
        near_at = source(place_ref[0], p, pieces)
        for c in range(chunks):
            bounds = row_bounds(place_ref, lengths_ref, range_ref, near_at, c)
            for f, (_, off) in enumerate(frame_slices(bounds, first, 1)):
                out_ref[p, c, f : f + 1, :] = off


def stats_kernel(place_ref, lengths_ref, range_ref, text_ref, *refs):
    kv_refs, all_ref, stats_scr = refs[:-2], refs[-2], refs[-1]
    chunks, near = text_ref.shape[0] * text_ref.shape[2] // CHUNK, len(kv_refs)
    stats_scr[...] = jnp.zeros_like(stats_scr)
    for c in range(chunks):
        q_c, g_c = chunk_of(text_ref, c, 0), chunk_of(text_ref, c, 1)
        bounds = row_bounds(place_ref, lengths_ref, range_ref, place_ref[0], c)
        parts = []
        for p, kv_ref in enumerate(kv_refs):
            first = (place_ref[4] + source(place_ref[0], p, near)) * FRAME_DEV
            parts.append(piece_stats(q_c, g_c, kv_ref, bounds, first))
        for k, part in enumerate(join(parts)):
            stats_scr[k * chunks + c : k * chunks + c + 1, :] = part
    stats = stats_scr[...]
    for k in range(all_ref.shape[0]):
        all_ref[k] = stats


def join_kernel(stats_ref, out_ref):
    lines = out_ref.shape[1] // 2
    parts = [
        [stats_ref[k, j * lines : (j + 1) * lines] for j in range(3)]
        for k in range(stats_ref.shape[0])
    ]
    top, total, weighted = join(parts)
    norm = jnp.concatenate((top + jnp.log2(total), weighted / total), axis=0)
    for k in range(out_ref.shape[0]):
        out_ref[k] = norm


def query_kernel(place_ref, lengths_ref, range_ref, text_ref, copies_ref, *refs):
    kv_refs, dq_ref, ds_scr = refs[:-2], refs[-2], refs[-1]
    norm_ref = copies_ref.at[0]
    chunks, near = norm_ref.shape[0] // 2, len(kv_refs)
    per = CHUNK // dq_ref.shape[1]
    for c in range(chunks):
        q_c, g_c = chunk_of(text_ref, c, 0), chunk_of(text_ref, c, 1)
        bounds = row_bounds(place_ref, lengths_ref, range_ref, place_ref[0], c)
        shift = norm_ref[c : c + 1, :]
        delta = norm_ref[chunks + c : chunks + c + 1, :]
        dq = jnp.zeros((HEAD_WIDTH, CHUNK), F32)
        for p, kv_ref in enumerate(kv_refs):
            rows = kv_ref.shape[1] // FRAME_DEV
            first = (place_ref[4] + source(place_ref[0], p, near)) * FRAME_DEV
            scores = dot(kv_ref[0], q_c, NT) * (SCALE * LOG2E)
            dprobs = dot(kv_ref[1], g_c, NT)
            for here, off in frame_slices(bounds, first, rows):
                probs = jnp.exp2(scores[here] - (shift + off))
                ds_scr[here] = (probs * (dprobs[here] - delta)).astype(BF16)
            dq += dot(kv_ref[0].T, ds_scr[...], NN)
        dq_ref[c * per : (c + 1) * per] = (dq * SCALE).T.reshape(per, dq_ref.shape[1], HEAD_WIDTH)


def token_kernel(place_ref, off_ref, kv_ref, norm_ref, far_vision_ref, *refs):
    pieces = norm_ref.shape[0]
    text_refs, out_refs = refs[:pieces], refs[pieces : 2 * pieces]
    p_scr, ds_scr, vision_ref, vision_sem = refs[2 * pieces :]
    parts = vision_sem.shape[0]
    width = vision_ref.shape[1] // parts
    copies = [
        pltpu.make_async_copy(
            far_vision_ref.at[:, p * width : (p + 1) * width],
            vision_ref.at[:, p * width : (p + 1) * width],
            vision_sem.at[p],
        )
        for p in range(parts)
    ]
    for copy in copies:
        copy.start()
    chunks = norm_ref.shape[1] // 2
    rows = kv_ref.shape[1] // FRAME_DEV
    key_sum = jnp.zeros(kv_ref.shape[1:], F32)
    value_sum = jnp.zeros(kv_ref.shape[1:], F32)
    for p, text_ref in enumerate(text_refs):
        near_at = source(place_ref[0], p, pieces)
        norm = norm_ref[near_at]
        for c in range(chunks):
            q_c, g_c = chunk_of(text_ref, c, 0), chunk_of(text_ref, c, 1)
            shift, delta = norm[c : c + 1], norm[chunks + c : chunks + c + 1]
            scores = dot(kv_ref[0], q_c, NT) * (SCALE * LOG2E)
            dprobs = dot(kv_ref[1], g_c, NT)
            for f in range(FRAME_DEV):
                here, off = slice(f * rows, (f + 1) * rows), off_ref[p, c, f : f + 1, :]
                probs = jnp.exp2(scores[here] - (shift + off))
                p_scr[here] = probs.astype(BF16)
                ds_scr[here] = (probs * (dprobs[here] - delta)).astype(BF16)
            value_sum += dot(p_scr[...], g_c, NN)
            key_sum += dot(ds_scr[...], q_c, NN)
    turned = jnp.concatenate(((key_sum * SCALE).T, value_sum.T), axis=0).astype(BF16)
    part = PART
    block = pieces * part
    for b in range(vision_ref.shape[1] // block):
        if b * block % width == 0:
            copies[b * block // width].wait()
        sums = dot(turned, vision_ref[:, b * block : (b + 1) * block], NN).T.astype(BF16)
        for m in range(pieces):

            @pl.when(place_ref[0] == m)
            def _(m=m, b=b, sums=sums):
                for x in range(pieces):
                    out_ref = out_refs[(x - m) % pieces]
                    out_ref[b * part : (b + 1) * part] = sums[x * part : (x + 1) * part]


def sum_kernel(parts_ref, out_ref):
    out_ref[...] = jnp.sum(parts_ref[...], axis=0).astype(BF16)


def shards(text_queries, text_grads, vision_keys, video_value_rows, vision, lengths, frame_range):
    far, near = lax.axis_size(FAR), lax.axis_size(NEAR)
    my_far, my_near = lax.axis_index(FAR), lax.axis_index(NEAR)
    peers = far * near
    own_rows = text_queries.shape[0]
    members = text_queries.shape[1] // HEAD_WIDTH
    lines = own_rows * members
    kv_rows = vision_keys.shape[0]
    features = vision.shape[1]
    place = jnp.stack(
        [
            my_near.astype(jnp.int32),
            jnp.int32(near),
            jnp.int32(own_rows),
            jnp.int32(lines),
            (my_far * near).astype(jnp.int32),
        ]
    )
    where = (place, lengths, frame_range)

    own_text = pl.pallas_call(
        prepare_kernel,
        out_shape=jax.ShapeDtypeStruct((far, 2, lines, HEAD_WIDTH), BF16),
        in_specs=[WHOLE] * 2,
        out_specs=WHOLE,
        compiler_params=PARAMS,
    )(text_queries, text_grads)
    own_kv = jnp.stack((vision_keys, video_value_rows))
    text = lax.all_to_all(own_text, FAR, 0, 0, tiled=True)
    all_kv = [own_kv] + [shifted(own_kv, NEAR, k) for k in range(1, near)]
    chunks = far * lines // CHUNK
    part = features // peers
    assert part == PART

    stats = pl.pallas_call(
        stats_kernel,
        out_shape=jax.ShapeDtypeStruct((far, STATS_LINES, CHUNK), F32),
        in_specs=[SCALARS] * 3 + [WHOLE] * (1 + near),
        out_specs=WHOLE,
        scratch_shapes=[pltpu.VMEM((STATS_LINES, CHUNK), F32)],
        compiler_params=PARAMS,
    )(*where, text, *all_kv)
    stats, text, where = lax.optimization_barrier((stats, text, where))
    stats = lax.all_to_all(stats, FAR, 0, 0, tiled=True)
    off = pl.pallas_call(
        mask_kernel,
        out_shape=jax.ShapeDtypeStruct((near, chunks, FRAME_DEV, CHUNK), F32),
        in_specs=[SCALARS] * 3,
        out_specs=WHOLE,
        compiler_params=PARAMS,
    )(*where)
    all_text = [text] + [shifted(text, NEAR, k) for k in range(1, near)]
    norms = pl.pallas_call(
        join_kernel,
        out_shape=jax.ShapeDtypeStruct((near, 2 * chunks, CHUNK), F32),
        in_specs=[WHOLE],
        out_specs=WHOLE,
        compiler_params=PARAMS,
    )(stats)
    all_norm = lax.all_to_all(norms, NEAR, 0, 0, tiled=True)

    dq = pl.pallas_call(
        query_kernel,
        out_shape=jax.ShapeDtypeStruct((far, lines, HEAD_WIDTH), F32),
        in_specs=[SCALARS] * 3 + [WHOLE] * (2 + near),
        out_specs=WHOLE,
        scratch_shapes=[pltpu.VMEM((kv_rows, CHUNK), BF16)],
        compiler_params=PARAMS,
    )(*where, text, norms, *all_kv)
    dq, all_norm = lax.optimization_barrier((dq, all_norm))
    dq = lax.all_to_all(dq, FAR, 0, 0, tiled=True)

    sums = pl.pallas_call(
        token_kernel,
        out_shape=[jax.ShapeDtypeStruct((far * part, 2 * HEAD_WIDTH), BF16)] * near,
        in_specs=[SCALARS]
        + [WHOLE] * 3
        + [pl.BlockSpec(memory_space=pltpu.HBM)]
        + [WHOLE] * near,
        out_specs=[WHOLE] * near,
        scratch_shapes=[
            pltpu.VMEM((kv_rows, CHUNK), BF16),
            pltpu.VMEM((kv_rows, CHUNK), BF16),
            pltpu.VMEM((kv_rows, features), BF16),
            pltpu.SemaphoreType.DMA((4,)),
        ],
        compiler_params=LARGE,
        cost_estimate=HEAVY,
    )(place, off, own_kv, all_norm, vision, *all_text)

    got = [sums[0]] + [shifted(sums[k], NEAR, k) for k in range(1, near)]

    dq = pl.pallas_call(
        sum_kernel,
        out_shape=jax.ShapeDtypeStruct((lines, HEAD_WIDTH), BF16),
        in_specs=[WHOLE],
        out_specs=WHOLE,
        compiler_params=PARAMS,
        cost_estimate=HEAVY,
    )(dq)
    dq = dq.reshape(members, own_rows, HEAD_WIDTH).transpose(1, 0, 2)
    dq = from_everyone(dq.reshape(own_rows, -1), FAR).reshape(far, own_rows, -1)

    weights = sum(one.astype(F32) for one in got).astype(BF16)
    weights, dq = lax.optimization_barrier((weights, dq))
    weights = lax.all_to_all(
        weights.reshape(far, part, 2 * HEAD_WIDTH), FAR, 0, 0, tiled=True
    )
    all_dq = [dq] + [shifted(dq, NEAR, k) for k in range(1, near)]
    query_grad = jnp.stack([lax.select_n(source(my_near, k, near), *all_dq) for k in range(near)], 1)
    query_grad = query_grad.reshape(peers * own_rows, -1)
    weights = jnp.sum(weights.astype(F32), axis=0)
    return query_grad, weights[:, :HEAD_WIDTH], weights[:, HEAD_WIDTH:]


def solution(mesh):
    finer = Mesh(
        mesh.devices.reshape(2, 8, 4, mesh.shape["head"]), ("tok_0", "tok_1", "tok_2", "head")
    )
    return jax.shard_map(
        shards,
        mesh=finer,
        in_specs=(
            P(TOK, "head"),
            P(TOK, "head"),
            P(TOK, "head"),
            P(TOK, "head"),
            P(TOK, None),
            P(),
            P(),
        ),
        out_specs=(P(None, "head"), P(TOK, "head"), P(TOK, "head")),
        check_vma=False,
    )
```

```python
import jax
import jax.numpy as jnp
from jax import lax
from jax.experimental import pallas as pl
from jax.experimental.pallas import tpu as pltpu
from jax.sharding import Mesh
from jax.sharding import PartitionSpec as P

HEAD_WIDTH = 128
FRAME_DEV = 4
TOK = ("tok_0", "tok_1", "tok_2")
FAR = ("tok_0", "tok_1")
NEAR = "tok_2"
CHUNK = 256
SCALE = HEAD_WIDTH**-0.5
LOG2E = 1.4426950408889634
OFF = 1e30
LOW = -1e29
F32 = jnp.float32
BF16 = jnp.bfloat16
NT = (((1,), (1,)), ((), ()))
NN = (((1,), (0,)), ((), ()))
PARAMS = pltpu.CompilerParams(vmem_limit_bytes=32 * 2**20)
LARGE = pltpu.CompilerParams(vmem_limit_bytes=52 * 2**20)
LARGER = pltpu.CompilerParams(vmem_limit_bytes=58 * 2**20)
WHOLE = pl.BlockSpec(memory_space=pltpu.VMEM)
SCALARS = pl.BlockSpec(memory_space=pltpu.SMEM)


def shifted(x, axis, step):
    peers = lax.axis_size(axis)
    return lax.ppermute(x, axis, [(i, (i + step) % peers) for i in range(peers)])


def dot(a, b, dims):
    return lax.dot_general(a, b, dims, preferred_element_type=F32)


def chunk_of(text_ref, near_at, c, which):
    per = CHUNK // text_ref.shape[3]
    return text_ref[c * per : (c + 1) * per, near_at, which].reshape(CHUNK, HEAD_WIDTH)


def row_bounds(place_ref, lengths_ref, range_ref, near_at, c):
    near, own_rows, lines = place_ref[1], place_ref[2], place_ref[3]
    line = lax.broadcasted_iota(jnp.int32, (1, CHUNK), 1) + c * CHUNK
    row = (lax.div(line, lines) * near + near_at) * own_rows + lax.rem(line, own_rows)
    begin = jnp.zeros((1, CHUNK), jnp.int32)
    end = jnp.zeros((1, CHUNK), jnp.int32)
    at = jnp.int32(0)
    for k in range(lengths_ref.shape[0]):
        stop = at + lengths_ref[k]
        inside = (row >= at) & (row < stop)
        begin = jnp.where(inside, range_ref[k, 0], begin)
        end = jnp.where(inside, range_ref[k, 1], end)
        at = stop
    return begin, end


def frame_offs(bounds, first):
    begin, end = bounds
    for f in range(FRAME_DEV):
        allowed = (begin <= first + f) & (end > first + f)
        yield jnp.where(allowed, 0.0, OFF).astype(F32)


def frame_slices(off_ref, rows):
    for f in range(FRAME_DEV):
        yield slice(f * rows, (f + 1) * rows), off_ref[f : f + 1, :]


def source(near_at, piece, near):
    return lax.rem(near_at + (near - piece), jnp.int32(near))


def join(parts):
    top = parts[0][0]
    for part in parts[1:]:
        top = jnp.maximum(top, part[0])
    total = jnp.zeros_like(top)
    weighted = jnp.zeros_like(top)
    for part in parts:
        factor = jnp.exp2(part[0] - top)
        total += part[1] * factor
        weighted += part[2] * factor
    return top, total, weighted


def piece_stats(q_c, g_c, kv_ref, off_ref):
    rows = kv_ref.shape[1] // FRAME_DEV
    scores = dot(kv_ref[0], q_c, NT) * (SCALE * LOG2E)
    dprobs = dot(kv_ref[1], g_c, NT)
    top = jnp.full((1, CHUNK), LOW, F32)
    for here, off in frame_slices(off_ref, rows):
        top = jnp.maximum(top, jnp.max(scores[here], axis=0, keepdims=True) - off)
    total = jnp.zeros((1, CHUNK), F32)
    weighted = jnp.zeros((1, CHUNK), F32)
    for here, off in frame_slices(off_ref, rows):
        terms = jnp.exp2(scores[here] - (top + off))
        total += jnp.sum(terms, axis=0, keepdims=True)
        weighted += jnp.sum(terms * dprobs[here], axis=0, keepdims=True)
    return top, total, weighted


def prepare_kernel(q_ref, g_ref, text_ref):
    members = q_ref.shape[1] // HEAD_WIDTH
    for which, ref in enumerate((q_ref, g_ref)):
        rows = ref[...].astype(F32)
        lines = jnp.concatenate(
            [rows[:, m * HEAD_WIDTH : (m + 1) * HEAD_WIDTH] for m in range(members)], axis=0
        ).astype(BF16)
        for k in range(text_ref.shape[0]):
            text_ref[k, which] = lines


def mask_kernel(place_ref, lengths_ref, range_ref, own_ref, all_ref):
    near, chunks = all_ref.shape[:2]
    base = place_ref[4]
    for c in range(chunks):
        bounds = row_bounds(place_ref, lengths_ref, range_ref, place_ref[0], c)
        for p in range(near):
            first = (base + source(place_ref[0], p, near)) * FRAME_DEV
            for f, off in enumerate(frame_offs(bounds, first)):
                own_ref[c, p, f : f + 1, :] = off
        for p in range(near):
            bounds = row_bounds(place_ref, lengths_ref, range_ref, p, c)
            first = (base + place_ref[0]) * FRAME_DEV
            for f, off in enumerate(frame_offs(bounds, first)):
                all_ref[p, c, f : f + 1, :] = off


def turn_kernel(vision_ref, out_ref):
    size = 256
    for at in range(0, out_ref.shape[0], size):
        out_ref[at : at + size] = vision_ref[:, at : at + size].T


def stats_kernel(place_ref, text_ref, off_ref, *refs):
    kv_refs, all_ref, stats_scr = refs[:-2], refs[-2], refs[-1]
    chunks = stats_scr.shape[0] // 3
    for c in range(chunks):
        q_c = chunk_of(text_ref, place_ref[0], c, 0)
        g_c = chunk_of(text_ref, place_ref[0], c, 1)
        parts = [
            piece_stats(q_c, g_c, kv_ref, off_ref.at[c, p]) for p, kv_ref in enumerate(kv_refs)
        ]
        for k, part in enumerate(join(parts)):
            stats_scr[k * chunks + c : k * chunks + c + 1, :] = part
    stats = stats_scr[...]
    for k in range(all_ref.shape[0]):
        all_ref[k] = stats


def join_kernel(stats_ref, out_ref):
    lines = stats_ref.shape[2] // 3
    for p in range(out_ref.shape[0]):
        parts = [
            [stats_ref[k, p, j * lines : (j + 1) * lines] for j in range(3)]
            for k in range(stats_ref.shape[0])
        ]
        top, total, weighted = join(parts)
        out_ref[p, :lines] = top + jnp.log2(total)
        out_ref[p, lines:] = weighted / total


def query_kernel(place_ref, text_ref, off_ref, norm_ref, *refs):
    kv_refs, dq_ref, ds_scr = refs[:-2], refs[-2], refs[-1]
    norm = norm_ref[place_ref[0]]
    chunks = norm.shape[0] // 2
    for c in range(chunks):
        q_c = chunk_of(text_ref, place_ref[0], c, 0)
        g_c = chunk_of(text_ref, place_ref[0], c, 1)
        shift, delta = norm[c : c + 1], norm[chunks + c : chunks + c + 1]
        dq = jnp.zeros((HEAD_WIDTH, CHUNK), F32)
        for p, kv_ref in enumerate(kv_refs):
            rows = kv_ref.shape[1] // FRAME_DEV
            scores = dot(kv_ref[0], q_c, NT) * (SCALE * LOG2E)
            dprobs = dot(kv_ref[1], g_c, NT)
            for here, off in frame_slices(off_ref.at[c, p], rows):
                probs = jnp.exp2(scores[here] - (shift + off))
                ds_scr[here] = (probs * (dprobs[here] - delta)).astype(BF16)
            dq += dot(kv_ref[0].T, ds_scr[...], NN)
        dq_ref[c * CHUNK : (c + 1) * CHUNK] = (dq * SCALE).T


def token_kernel(text_ref, off_ref, kv_ref, norm_ref, far_vision_ref, out_ref, *refs):
    p_scr, ds_scr, kv_scr, vision_ref, vision_sem = refs
    parts = vision_sem.shape[0]
    size = vision_ref.shape[0] // parts
    copies = [
        pltpu.make_async_copy(
            far_vision_ref.at[p * size : (p + 1) * size],
            vision_ref.at[p * size : (p + 1) * size],
            vision_sem.at[p],
        )
        for p in range(parts)
    ]
    for copy in copies:
        copy.start()
    pieces, chunks = off_ref.shape[:2]
    rows = kv_ref.shape[1] // FRAME_DEV
    key_sum = jnp.zeros(kv_ref.shape[1:], F32)
    value_sum = jnp.zeros(kv_ref.shape[1:], F32)
    for p in range(pieces):
        for c in range(chunks):
            q_c, g_c = chunk_of(text_ref, p, c, 0), chunk_of(text_ref, p, c, 1)
            shift = norm_ref[p, c : c + 1, :]
            delta = norm_ref[p, chunks + c : chunks + c + 1, :]
            scores = dot(kv_ref[0], q_c, NT) * (SCALE * LOG2E)
            dprobs = dot(kv_ref[1], g_c, NT)
            for here, off in frame_slices(off_ref.at[p, c], rows):
                probs = jnp.exp2(scores[here] - (shift + off))
                p_scr[here] = probs.astype(BF16)
                ds_scr[here] = (probs * (dprobs[here] - delta)).astype(BF16)
            value_sum += dot(p_scr[...], g_c, NN)
            key_sum += dot(ds_scr[...], q_c, NN)
    kv_scr[:, :HEAD_WIDTH] = (key_sum * SCALE).astype(BF16)
    kv_scr[:, HEAD_WIDTH:] = value_sum.astype(BF16)
    block = 512
    for at in range(0, out_ref.shape[0], block):
        if at % size == 0:
            copies[at // size].wait()
        out_ref[at : at + block] = dot(vision_ref[at : at + block], kv_scr[...], NN).astype(BF16)


def partner_sum(x, axis, step, kind):
    peers = lax.axis_size(axis)
    sent = x.astype(kind)
    got = lax.ppermute(sent, axis, [(i, i ^ step) for i in range(peers)])
    return sent.astype(F32) + got.astype(F32)


def shards(text_queries, text_grads, vision_keys, video_value_rows, vision, lengths, frame_range):
    far, near = lax.axis_size(FAR), lax.axis_size(NEAR)
    my_far, my_near = lax.axis_index(FAR), lax.axis_index(NEAR)
    peers = far * near
    own_rows = text_queries.shape[0]
    members = text_queries.shape[1] // HEAD_WIDTH
    lines = own_rows * members
    kv_rows = vision_keys.shape[0]
    features = vision.shape[1]
    place = jnp.stack(
        [
            my_near.astype(jnp.int32),
            jnp.int32(near),
            jnp.int32(own_rows),
            jnp.int32(lines),
            (my_far * near).astype(jnp.int32),
        ]
    )
    chunks = far * lines // CHUNK
    own_text = pl.pallas_call(
        prepare_kernel,
        out_shape=jax.ShapeDtypeStruct((peers, 2, lines, HEAD_WIDTH), BF16),
        in_specs=[WHOLE] * 2,
        out_specs=WHOLE,
        compiler_params=PARAMS,
    )(text_queries, text_grads)
    text = lax.all_to_all(own_text, TOK, 0, 0, tiled=True)
    text = text.reshape(far, near, 2, lines, HEAD_WIDTH)
    own_kv = jnp.stack((vision_keys, video_value_rows))
    all_kv = [own_kv] + [shifted(own_kv, NEAR, k) for k in range(1, near)]

    own_off, all_off = pl.pallas_call(
        mask_kernel,
        out_shape=(
            jax.ShapeDtypeStruct((chunks, near, FRAME_DEV, CHUNK), F32),
            jax.ShapeDtypeStruct((near, chunks, FRAME_DEV, CHUNK), F32),
        ),
        in_specs=[SCALARS] * 3,
        out_specs=(WHOLE, WHOLE),
        compiler_params=PARAMS,
    )(place, lengths, frame_range)
    turned = pl.pallas_call(
        turn_kernel,
        out_shape=jax.ShapeDtypeStruct((features, kv_rows), BF16),
        grid=(4,),
        in_specs=[pl.BlockSpec((kv_rows, features // 4), lambda i: (0, i))],
        out_specs=pl.BlockSpec((features // 4, kv_rows), lambda i: (i, 0)),
        compiler_params=LARGER,
    )(vision)
    text, turned, all_off = lax.optimization_barrier((text, turned, all_off))

    stats = pl.pallas_call(
        stats_kernel,
        out_shape=jax.ShapeDtypeStruct((peers, 3 * chunks, CHUNK), F32),
        in_specs=[SCALARS] + [WHOLE] * (2 + near),
        out_specs=WHOLE,
        scratch_shapes=[pltpu.VMEM((3 * chunks, CHUNK), F32)],
        compiler_params=PARAMS,
    )(place, text, own_off, *all_kv)
    stats = lax.all_to_all(stats, TOK, 0, 0, tiled=True)
    norm = pl.pallas_call(
        join_kernel,
        out_shape=jax.ShapeDtypeStruct((near, 2 * chunks, CHUNK), F32),
        in_specs=[WHOLE],
        out_specs=WHOLE,
        compiler_params=PARAMS,
    )(stats.reshape(far, near, 3 * chunks, CHUNK))

    sums = pl.pallas_call(
        token_kernel,
        out_shape=jax.ShapeDtypeStruct((features, 2 * HEAD_WIDTH), BF16),
        in_specs=[WHOLE] * 4 + [pl.BlockSpec(memory_space=pltpu.HBM)],
        out_specs=WHOLE,
        scratch_shapes=[
            pltpu.VMEM((kv_rows, CHUNK), BF16),
            pltpu.VMEM((kv_rows, CHUNK), BF16),
            pltpu.VMEM((kv_rows, 2 * HEAD_WIDTH), BF16),
            pltpu.VMEM((features, kv_rows), BF16),
            pltpu.SemaphoreType.DMA((4,)),
        ],
        compiler_params=LARGE,
    )(text, all_off, own_kv, norm, turned)
    sums, norm = lax.optimization_barrier((sums, norm))
    weights = lax.all_to_all(
        sums.reshape(peers, features // peers, 2 * HEAD_WIDTH), TOK, 0, 0, tiled=True
    )
    weights = jnp.sum(weights.astype(F32), axis=0)

    dq = pl.pallas_call(
        query_kernel,
        out_shape=jax.ShapeDtypeStruct((far * lines, HEAD_WIDTH), F32),
        in_specs=[SCALARS] + [WHOLE] * (3 + near),
        out_specs=WHOLE,
        scratch_shapes=[pltpu.VMEM((kv_rows, CHUNK), BF16)],
        compiler_params=PARAMS,
    )(place, text, own_off, norm, *all_kv)
    dq = partner_sum(dq, "tok_1", 1, F32)
    dq = partner_sum(dq, "tok_1", 2, BF16)
    dq = partner_sum(dq, "tok_1", 4, BF16)
    dq = partner_sum(dq, "tok_0", 1, BF16)
    dq = dq.astype(BF16).reshape(far, members, own_rows, HEAD_WIDTH)
    dq = dq.transpose(0, 2, 1, 3).reshape(far, own_rows, members * HEAD_WIDTH)
    all_dq = [dq] + [shifted(dq, NEAR, k) for k in range(1, near)]
    query_grad = jnp.stack(
        [lax.select_n(source(my_near, k, near), *all_dq) for k in range(near)], 1
    )
    query_grad = query_grad.reshape(peers * own_rows, -1)
    return query_grad, weights[:, :HEAD_WIDTH], weights[:, HEAD_WIDTH:]


def solution(mesh):
    finer = Mesh(
        mesh.devices.reshape(2, 8, 4, mesh.shape["head"]), ("tok_0", "tok_1", "tok_2", "head")
    )
    return jax.shard_map(
        shards,
        mesh=finer,
        in_specs=(
            P(TOK, "head"),
            P(TOK, "head"),
            P(TOK, "head"),
            P(TOK, "head"),
            P(TOK, None),
            P(),
            P(),
        ),
        out_specs=(P(None, "head"), P(TOK, "head"), P(TOK, "head")),
        check_vma=False,
    )
```

```python
import jax
import jax.numpy as jnp
from jax import lax
from jax.experimental import pallas as pl
from jax.experimental.pallas import tpu as pltpu
from jax.sharding import Mesh
from jax.sharding import PartitionSpec as P

HEAD_WIDTH = 128
FRAME_DEV = 4
TOK = ("tok_0", "tok_1", "tok_2")
FAR = ("tok_0", "tok_1")
NEAR = "tok_2"
CHUNK = 256
SCALE = HEAD_WIDTH**-0.5
LOG2E = 1.4426950408889634
OFF = 1e30
LOW = -1e29
F32 = jnp.float32
BF16 = jnp.bfloat16
NT = (((1,), (1,)), ((), ()))
NN = (((1,), (0,)), ((), ()))
PARAMS = pltpu.CompilerParams(vmem_limit_bytes=32 * 2**20)
LARGE = pltpu.CompilerParams(vmem_limit_bytes=52 * 2**20)
LARGER = pltpu.CompilerParams(vmem_limit_bytes=58 * 2**20)
HEAVY = pl.CostEstimate(flops=10**11, bytes_accessed=2**20, transcendentals=0)
WHOLE = pl.BlockSpec(memory_space=pltpu.VMEM)
SCALARS = pl.BlockSpec(memory_space=pltpu.SMEM)


def from_everyone(x, axis):
    peers = lax.axis_size(axis)
    return lax.all_to_all(jnp.broadcast_to(x[None], (peers, *x.shape)), axis, 0, 0, tiled=True)


def shifted(x, axis, step):
    peers = lax.axis_size(axis)
    return lax.ppermute(x, axis, [(i, (i + step) % peers) for i in range(peers)])


def dot(a, b, dims):
    return lax.dot_general(a, b, dims, preferred_element_type=F32)


def chunk_of(text_ref, c, which):
    per = CHUNK // text_ref.shape[2]
    return text_ref[c * per : (c + 1) * per, which].reshape(CHUNK, HEAD_WIDTH)


def frame_slices(off_ref, c, rows, frames):
    for f in range(frames):
        yield slice(f * rows, (f + 1) * rows), off_ref[c, f : f + 1, :]


def join(parts):
    top = parts[0][0]
    for part in parts[1:]:
        top = jnp.maximum(top, part[0])
    total = jnp.zeros_like(top)
    weighted = jnp.zeros_like(top)
    for part in parts:
        factor = jnp.exp2(part[0] - top)
        total += part[1] * factor
        weighted += part[2] * factor
    return top, total, weighted


def piece_stats(q_c, g_c, kv_ref, off_ref, c):
    rows = kv_ref.shape[1] // FRAME_DEV
    scores = dot(kv_ref[0], q_c, NT) * (SCALE * LOG2E)
    dprobs = dot(kv_ref[1], g_c, NT)
    top = jnp.full((1, CHUNK), LOW, F32)
    for here, off in frame_slices(off_ref, c, rows, FRAME_DEV):
        top = jnp.maximum(top, jnp.max(scores[here], axis=0, keepdims=True) - off)
    total = jnp.zeros((1, CHUNK), F32)
    weighted = jnp.zeros((1, CHUNK), F32)
    for here, off in frame_slices(off_ref, c, rows, FRAME_DEV):
        terms = jnp.exp2(scores[here] - (top + off))
        total += jnp.sum(terms, axis=0, keepdims=True)
        weighted += jnp.sum(terms * dprobs[here], axis=0, keepdims=True)
    return top, total, weighted


def stats_kernel(text_ref, off_ref, *refs):
    kv_refs, all_ref, stats_scr = refs[:-2], refs[-2], refs[-1]
    chunks = stats_scr.shape[0] // 3
    for c in range(chunks):
        q_c, g_c = chunk_of(text_ref, c, 0), chunk_of(text_ref, c, 1)
        parts = []
        for p, kv_ref in enumerate(kv_refs):
            offs = off_ref.at[:, p * FRAME_DEV : (p + 1) * FRAME_DEV]
            parts.append(piece_stats(q_c, g_c, kv_ref, offs, c))
        for k, part in enumerate(join(parts)):
            stats_scr[k * chunks + c : k * chunks + c + 1, :] = part
    stats = stats_scr[...]
    for k in range(all_ref.shape[0]):
        all_ref[k] = stats


def join_kernel(stats_ref, out_ref):
    lines = stats_ref.shape[1] // 3
    parts = [
        [stats_ref[k, j * lines : (j + 1) * lines] for j in range(3)]
        for k in range(stats_ref.shape[0])
    ]
    top, total, weighted = join(parts)
    norm = jnp.concatenate((top + jnp.log2(total), weighted / total), axis=0)
    for k in range(out_ref.shape[0]):
        out_ref[k] = norm


def query_kernel(text_ref, off_ref, copies_ref, *refs):
    kv_refs, dq_ref, ds_scr = refs[:-2], refs[-2], refs[-1]
    norm_ref = copies_ref.at[0]
    chunks = norm_ref.shape[0] // 2
    per = CHUNK // dq_ref.shape[1]
    for c in range(chunks):
        q_c, g_c = chunk_of(text_ref, c, 0), chunk_of(text_ref, c, 1)
        shift = norm_ref[c : c + 1, :]
        delta = norm_ref[chunks + c : chunks + c + 1, :]
        dq = jnp.zeros((HEAD_WIDTH, CHUNK), F32)
        for p, kv_ref in enumerate(kv_refs):
            rows = kv_ref.shape[1] // FRAME_DEV
            scores = dot(kv_ref[0], q_c, NT) * (SCALE * LOG2E)
            dprobs = dot(kv_ref[1], g_c, NT)
            offs = off_ref.at[:, p * FRAME_DEV : (p + 1) * FRAME_DEV]
            for here, off in frame_slices(offs, c, rows, FRAME_DEV):
                probs = jnp.exp2(scores[here] - (shift + off))
                ds_scr[here] = (probs * (dprobs[here] - delta)).astype(BF16)
            dq += dot(kv_ref[0].T, ds_scr[...], NN)
        dq_ref[c * per : (c + 1) * per] = (dq * SCALE).T.reshape(per, dq_ref.shape[1], HEAD_WIDTH)


def token_kernel(near_ref, kv_ref, off_ref, norm_ref, far_vision_ref, *refs):
    pieces = off_ref.shape[0]
    text_refs, out_refs = refs[:pieces], refs[pieces : 2 * pieces]
    p_scr, ds_scr, kv_scr, vision_ref, vision_sem = refs[2 * pieces :]
    copies = [
        pltpu.make_async_copy(far_vision_ref.at[p], vision_ref.at[p], vision_sem.at[p])
        for p in range(pieces)
    ]
    for copy in copies:
        copy.start()
    chunks = norm_ref.shape[1] // 2
    rows = kv_ref.shape[1] // FRAME_DEV
    key_sum = jnp.zeros(kv_ref.shape[1:], F32)
    value_sum = jnp.zeros(kv_ref.shape[1:], F32)
    for p, text_ref in enumerate(text_refs):
        norm = norm_ref[(near_ref[0] + (pieces - p)) % pieces]
        for c in range(chunks):
            q_c, g_c = chunk_of(text_ref, c, 0), chunk_of(text_ref, c, 1)
            shift, delta = norm[c : c + 1], norm[chunks + c : chunks + c + 1]
            scores = dot(kv_ref[0], q_c, NT) * (SCALE * LOG2E)
            dprobs = dot(kv_ref[1], g_c, NT)
            for here, off in frame_slices(off_ref.at[p], c, rows, FRAME_DEV):
                probs = jnp.exp2(scores[here] - (shift + off))
                p_scr[here] = probs.astype(BF16)
                ds_scr[here] = (probs * (dprobs[here] - delta)).astype(BF16)
            value_sum += dot(p_scr[...], g_c, NN)
            key_sum += dot(ds_scr[...], q_c, NN)
    kv_scr[:, :HEAD_WIDTH] = (key_sum * SCALE).astype(BF16)
    kv_scr[:, HEAD_WIDTH:] = value_sum.astype(BF16)
    size = 512
    for p, out_ref in enumerate(out_refs):
        copies[p].wait()
        for at in range(0, out_ref.shape[0], size):
            block = vision_ref[p, at : at + size]
            out_ref[at : at + size] = dot(block, kv_scr[...], NN).astype(BF16)


def sum_kernel(parts_ref, out_ref):
    out_ref[...] = jnp.sum(parts_ref[...], axis=0).astype(BF16)


def turn_kernel(near_ref, vision_ref, out_ref):
    pieces, deep, size, _ = out_ref.shape
    for d in range(deep):
        turned = vision_ref[:, d * pieces * size : (d + 1) * pieces * size].T
        for p in range(pieces):
            at = lax.rem(p + pieces - near_ref[0], pieces)
            out_ref[at, d] = turned[p * size : (p + 1) * size]


def bases_from(at, peers):
    return [lax.rem(at + peers - k, jnp.int32(peers)) for k in range(peers)]


def row_bounds(lengths, frame_range, rows):
    part_ids = jnp.arange(lengths.shape[0], dtype=jnp.int32)
    ends = jnp.sum(jnp.where(part_ids[None, :] <= part_ids[:, None], lengths[None, :], 0), axis=1)
    segment = jnp.sum((rows[:, None] >= ends[None, :]).astype(jnp.int32), axis=1)
    pick = (segment[:, None] == part_ids[None, :]).astype(jnp.int32)
    begin = jnp.sum(pick * frame_range[None, :, 0], axis=1)
    end = jnp.sum(pick * frame_range[None, :, 1], axis=1)
    return begin, end


def offsets(begin, end, at):
    allowed = (at[:, None] >= begin[None, :]) & (at[:, None] < end[None, :])
    off = jnp.where(allowed, 0.0, OFF).astype(F32)
    return off.reshape(at.shape[0], -1, CHUNK).transpose(1, 0, 2)


def shards(text_queries, text_grads, vision_keys, video_value_rows, vision, lengths, frame_range):
    far, near = lax.axis_size(FAR), lax.axis_size(NEAR)
    my_far, my_near = lax.axis_index(FAR), lax.axis_index(NEAR)
    peers = far * near
    own_rows = text_queries.shape[0]
    members = text_queries.shape[1] // HEAD_WIDTH
    lines = own_rows * members
    kv_rows = vision_keys.shape[0]
    features = vision.shape[1]
    near_id = my_near.reshape(1).astype(jnp.int32)

    own_text = jnp.stack(
        (text_queries.reshape(lines, HEAD_WIDTH), text_grads.reshape(lines, HEAD_WIDTH))
    )
    own_text = jnp.broadcast_to(own_text[None], (far, *own_text.shape))
    own_text, vision_keys, video_value_rows = lax.optimization_barrier(
        (own_text, vision_keys, video_value_rows)
    )
    text = lax.all_to_all(own_text, FAR, 0, 0, tiled=True)
    own_kv = jnp.stack((vision_keys, video_value_rows))
    all_kv = [own_kv] + [shifted(own_kv, NEAR, k) for k in range(1, near)]
    all_text = [text] + [shifted(text, NEAR, k) for k in range(1, near)]

    line_ids = jnp.arange(far * lines, dtype=jnp.int32)
    sources = jnp.stack(bases_from(my_near, near))
    row_of = (
        (line_ids // lines)[None, :] * (near * own_rows)
        + sources[:, None] * own_rows
        + (line_ids % lines // members)[None, :]
    )
    begin, end = row_bounds(lengths, frame_range, row_of.reshape(-1))
    steps = jnp.arange(FRAME_DEV, dtype=jnp.int32)
    first = (my_far * near + sources) * FRAME_DEV
    group_frames = (first[:, None] + steps[None, :]).reshape(-1)
    own_off = offsets(begin[: far * lines], end[: far * lines], group_frames)
    all_off = offsets(begin, end, first[0] + steps)
    chunks = far * lines // CHUNK
    all_off = all_off.reshape(near, chunks, FRAME_DEV, CHUNK)

    part = features // peers
    turned = pl.pallas_call(
        turn_kernel,
        out_shape=jax.ShapeDtypeStruct((near, far, part, kv_rows), BF16),
        grid=(far // 4,),
        in_specs=[SCALARS, pl.BlockSpec((kv_rows, 4 * near * part), lambda i: (0, i))],
        out_specs=pl.BlockSpec((near, 4, part, kv_rows), lambda i: (0, i, 0, 0)),
        compiler_params=LARGER,
    )(near_id, vision)
    turned = turned.reshape(near, far * part, kv_rows)
    text, turned = lax.optimization_barrier((text, turned))

    stats = pl.pallas_call(
        stats_kernel,
        out_shape=jax.ShapeDtypeStruct((far, 3 * chunks, CHUNK), F32),
        in_specs=[WHOLE] * (2 + near),
        out_specs=WHOLE,
        scratch_shapes=[pltpu.VMEM((3 * chunks, CHUNK), F32)],
        compiler_params=PARAMS,
    )(text, own_off, *all_kv)
    stats = lax.all_to_all(stats, FAR, 0, 0, tiled=True)
    norms = pl.pallas_call(
        join_kernel,
        out_shape=jax.ShapeDtypeStruct((near, 2 * chunks, CHUNK), F32),
        in_specs=[WHOLE],
        out_specs=WHOLE,
        compiler_params=PARAMS,
    )(stats)
    all_norm = lax.all_to_all(norms, NEAR, 0, 0, tiled=True)

    dq = pl.pallas_call(
        query_kernel,
        out_shape=jax.ShapeDtypeStruct((far, lines, HEAD_WIDTH), F32),
        in_specs=[WHOLE] * (3 + near),
        out_specs=WHOLE,
        scratch_shapes=[pltpu.VMEM((kv_rows, CHUNK), BF16)],
        compiler_params=PARAMS,
    )(text, own_off, norms, *all_kv)
    dq, all_norm = lax.optimization_barrier((dq, all_norm))
    dq = lax.all_to_all(dq, FAR, 0, 0, tiled=True)

    sums = pl.pallas_call(
        token_kernel,
        out_shape=[jax.ShapeDtypeStruct((far * part, 2 * HEAD_WIDTH), BF16)] * near,
        in_specs=[SCALARS] + [WHOLE] * 3 + [pl.BlockSpec(memory_space=pltpu.HBM)] + [WHOLE] * near,
        out_specs=[WHOLE] * near,
        scratch_shapes=[
            pltpu.VMEM((kv_rows, CHUNK), BF16),
            pltpu.VMEM((kv_rows, CHUNK), BF16),
            pltpu.VMEM((kv_rows, 2 * HEAD_WIDTH), BF16),
            pltpu.VMEM((near, far * part, kv_rows), BF16),
            pltpu.SemaphoreType.DMA((near,)),
        ],
        compiler_params=LARGE,
        cost_estimate=HEAVY,
    )(near_id, own_kv, all_off, all_norm, turned, *all_text)

    got = [sums[0]] + [shifted(sums[k], NEAR, k) for k in range(1, near)]

    dq = pl.pallas_call(
        sum_kernel,
        out_shape=jax.ShapeDtypeStruct((lines, HEAD_WIDTH), BF16),
        in_specs=[WHOLE],
        out_specs=WHOLE,
        compiler_params=PARAMS,
        cost_estimate=HEAVY,
    )(dq)
    dq = from_everyone(dq.reshape(own_rows, -1), FAR).reshape(far, own_rows, -1)

    weights = sum(one.astype(F32) for one in got).astype(BF16)
    weights, dq = lax.optimization_barrier((weights, dq))
    weights = lax.all_to_all(
        weights.reshape(far, part, 2 * HEAD_WIDTH), FAR, 0, 0, tiled=True
    )
    all_dq = [dq] + [shifted(dq, NEAR, k) for k in range(1, near)]
    query_grad = jnp.stack([lax.select_n(base, *all_dq) for base in bases_from(my_near, near)], 1)
    query_grad = query_grad.reshape(peers * own_rows, -1)
    weights = jnp.sum(weights.astype(F32), axis=0)
    return query_grad, weights[:, :HEAD_WIDTH], weights[:, HEAD_WIDTH:]


def solution(mesh):
    finer = Mesh(
        mesh.devices.reshape(2, 8, 4, mesh.shape["head"]), ("tok_0", "tok_1", "tok_2", "head")
    )
    return jax.shard_map(
        shards,
        mesh=finer,
        in_specs=(
            P(TOK, "head"),
            P(TOK, "head"),
            P(TOK, "head"),
            P(TOK, "head"),
            P(TOK, None),
            P(),
            P(),
        ),
        out_specs=(P(None, "head"), P(TOK, "head"), P(TOK, "head")),
        check_vma=False,
    )
```

```python
import jax
import jax.numpy as jnp
from jax import lax
from jax.experimental import pallas as pl
from jax.experimental.pallas import tpu as pltpu
from jax.sharding import Mesh
from jax.sharding import PartitionSpec as P

HEAD_WIDTH = 128
FRAME_DEV = 4
TOK = ("tok_0", "tok_1", "tok_2")
FAR = ("tok_0", "tok_1")
NEAR = "tok_2"
CHUNK = 256
SCALE = HEAD_WIDTH**-0.5
LOG2E = 1.4426950408889634
OFF = 1e30
LOW = -1e29
F32 = jnp.float32
BF16 = jnp.bfloat16
NT = (((1,), (1,)), ((), ()))
NN = (((1,), (0,)), ((), ()))
PARAMS = pltpu.CompilerParams(vmem_limit_bytes=32 * 2**20)
LARGE = pltpu.CompilerParams(vmem_limit_bytes=52 * 2**20)
LARGER = pltpu.CompilerParams(vmem_limit_bytes=58 * 2**20)
HEAVY = pl.CostEstimate(flops=10**11, bytes_accessed=2**20, transcendentals=0)
WHOLE = pl.BlockSpec(memory_space=pltpu.VMEM)
SCALARS = pl.BlockSpec(memory_space=pltpu.SMEM)


def from_everyone(x, axis):
    peers = lax.axis_size(axis)
    return lax.all_to_all(jnp.broadcast_to(x[None], (peers, *x.shape)), axis, 0, 0, tiled=True)


def shifted(x, axis, step):
    peers = lax.axis_size(axis)
    return lax.ppermute(x, axis, [(i, (i + step) % peers) for i in range(peers)])


def dot(a, b, dims):
    return lax.dot_general(a, b, dims, preferred_element_type=F32)


def chunk_of(text_ref, c, which):
    per = CHUNK // text_ref.shape[2]
    return text_ref[c * per : (c + 1) * per, which].reshape(CHUNK, HEAD_WIDTH)


def frame_slices(off_ref, c, rows, frames):
    for f in range(frames):
        yield slice(f * rows, (f + 1) * rows), off_ref[c, f : f + 1, :]


def join(parts):
    top = parts[0][0]
    for part in parts[1:]:
        top = jnp.maximum(top, part[0])
    total = jnp.zeros_like(top)
    weighted = jnp.zeros_like(top)
    for part in parts:
        factor = jnp.exp2(part[0] - top)
        total += part[1] * factor
        weighted += part[2] * factor
    return top, total, weighted


def piece_stats(q_c, g_c, kv_ref, off_ref, c):
    rows = kv_ref.shape[1] // FRAME_DEV
    scores = dot(kv_ref[0], q_c, NT) * (SCALE * LOG2E)
    dprobs = dot(kv_ref[1], g_c, NT)
    top = jnp.full((1, CHUNK), LOW, F32)
    for here, off in frame_slices(off_ref, c, rows, FRAME_DEV):
        top = jnp.maximum(top, jnp.max(scores[here], axis=0, keepdims=True) - off)
    total = jnp.zeros((1, CHUNK), F32)
    weighted = jnp.zeros((1, CHUNK), F32)
    for here, off in frame_slices(off_ref, c, rows, FRAME_DEV):
        terms = jnp.exp2(scores[here] - (top + off))
        total += jnp.sum(terms, axis=0, keepdims=True)
        weighted += jnp.sum(terms * dprobs[here], axis=0, keepdims=True)
    return top, total, weighted


def stats_kernel(text_ref, off_ref, *refs):
    kv_refs, all_ref, stats_scr = refs[:-2], refs[-2], refs[-1]
    chunks = stats_scr.shape[0] // 3
    for c in range(chunks):
        q_c, g_c = chunk_of(text_ref, c, 0), chunk_of(text_ref, c, 1)
        parts = []
        for p, kv_ref in enumerate(kv_refs):
            offs = off_ref.at[:, p * FRAME_DEV : (p + 1) * FRAME_DEV]
            parts.append(piece_stats(q_c, g_c, kv_ref, offs, c))
        for k, part in enumerate(join(parts)):
            stats_scr[k * chunks + c : k * chunks + c + 1, :] = part
    stats = stats_scr[...]
    for k in range(all_ref.shape[0]):
        all_ref[k] = stats


def join_kernel(stats_ref, out_ref):
    lines = stats_ref.shape[1] // 3
    parts = [
        [stats_ref[k, j * lines : (j + 1) * lines] for j in range(3)]
        for k in range(stats_ref.shape[0])
    ]
    top, total, weighted = join(parts)
    norm = jnp.concatenate((top + jnp.log2(total), weighted / total), axis=0)
    for k in range(out_ref.shape[0]):
        out_ref[k] = norm


def query_kernel(text_ref, off_ref, copies_ref, *refs):
    kv_refs, dq_ref, ds_scr = refs[:-2], refs[-2], refs[-1]
    norm_ref = copies_ref.at[0]
    chunks = norm_ref.shape[0] // 2
    per = CHUNK // dq_ref.shape[1]
    for c in range(chunks):
        q_c, g_c = chunk_of(text_ref, c, 0), chunk_of(text_ref, c, 1)
        shift = norm_ref[c : c + 1, :]
        delta = norm_ref[chunks + c : chunks + c + 1, :]
        dq = jnp.zeros((HEAD_WIDTH, CHUNK), F32)
        for p, kv_ref in enumerate(kv_refs):
            rows = kv_ref.shape[1] // FRAME_DEV
            scores = dot(kv_ref[0], q_c, NT) * (SCALE * LOG2E)
            dprobs = dot(kv_ref[1], g_c, NT)
            offs = off_ref.at[:, p * FRAME_DEV : (p + 1) * FRAME_DEV]
            for here, off in frame_slices(offs, c, rows, FRAME_DEV):
                probs = jnp.exp2(scores[here] - (shift + off))
                ds_scr[here] = (probs * (dprobs[here] - delta)).astype(BF16)
            dq += dot(kv_ref[0].T, ds_scr[...], NN)
        dq = (dq * SCALE).T.reshape(per, dq_ref.shape[1], HEAD_WIDTH)
        dq_ref[c * per : (c + 1) * per] = dq.astype(BF16)


def token_kernel(near_ref, kv_ref, off_ref, norm_ref, far_vision_ref, *refs):
    pieces = off_ref.shape[0]
    text_refs, out_refs = refs[:pieces], refs[pieces : 2 * pieces]
    p_scr, ds_scr, kv_scr, vision_ref, vision_sem = refs[2 * pieces :]
    copies = [
        pltpu.make_async_copy(far_vision_ref.at[p], vision_ref.at[p], vision_sem.at[p])
        for p in range(pieces)
    ]
    for copy in copies:
        copy.start()
    chunks = norm_ref.shape[1] // 2
    rows = kv_ref.shape[1] // FRAME_DEV
    key_sum = jnp.zeros(kv_ref.shape[1:], F32)
    value_sum = jnp.zeros(kv_ref.shape[1:], F32)
    for p, text_ref in enumerate(text_refs):
        norm = norm_ref[(near_ref[0] + (pieces - p)) % pieces]
        for c in range(chunks):
            q_c, g_c = chunk_of(text_ref, c, 0), chunk_of(text_ref, c, 1)
            shift, delta = norm[c : c + 1], norm[chunks + c : chunks + c + 1]
            scores = dot(kv_ref[0], q_c, NT) * (SCALE * LOG2E)
            dprobs = dot(kv_ref[1], g_c, NT)
            for here, off in frame_slices(off_ref.at[p], c, rows, FRAME_DEV):
                probs = jnp.exp2(scores[here] - (shift + off))
                p_scr[here] = probs.astype(BF16)
                ds_scr[here] = (probs * (dprobs[here] - delta)).astype(BF16)
            value_sum += dot(p_scr[...], g_c, NN)
            key_sum += dot(ds_scr[...], q_c, NN)
    kv_scr[:, :HEAD_WIDTH] = (key_sum * SCALE).astype(BF16)
    kv_scr[:, HEAD_WIDTH:] = value_sum.astype(BF16)
    size = 512
    for p, out_ref in enumerate(out_refs):
        copies[p].wait()
        for at in range(0, out_ref.shape[0], size):
            block = vision_ref[p, at : at + size]
            out_ref[at : at + size] = dot(block, kv_scr[...], NN).astype(BF16)


def sum_kernel(parts_ref, out_ref):
    out_ref[...] = jnp.sum(parts_ref[...].astype(F32), axis=0).astype(BF16)


def turn_kernel(near_ref, vision_ref, out_ref):
    pieces, deep, size, _ = out_ref.shape
    for d in range(deep):
        turned = vision_ref[:, d * pieces * size : (d + 1) * pieces * size].T
        for p in range(pieces):
            at = lax.rem(p + pieces - near_ref[0], pieces)
            out_ref[at, d] = turned[p * size : (p + 1) * size]


def bases_from(at, peers):
    return [lax.rem(at + peers - k, jnp.int32(peers)) for k in range(peers)]


def row_bounds(lengths, frame_range, rows):
    part_ids = jnp.arange(lengths.shape[0], dtype=jnp.int32)
    ends = jnp.sum(jnp.where(part_ids[None, :] <= part_ids[:, None], lengths[None, :], 0), axis=1)
    segment = jnp.sum((rows[:, None] >= ends[None, :]).astype(jnp.int32), axis=1)
    pick = (segment[:, None] == part_ids[None, :]).astype(jnp.int32)
    begin = jnp.sum(pick * frame_range[None, :, 0], axis=1)
    end = jnp.sum(pick * frame_range[None, :, 1], axis=1)
    return begin, end


def offsets(begin, end, at):
    allowed = (at[:, None] >= begin[None, :]) & (at[:, None] < end[None, :])
    off = jnp.where(allowed, 0.0, OFF).astype(F32)
    return off.reshape(at.shape[0], -1, CHUNK).transpose(1, 0, 2)


def shards(text_queries, text_grads, vision_keys, video_value_rows, vision, lengths, frame_range):
    far, near = lax.axis_size(FAR), lax.axis_size(NEAR)
    my_far, my_near = lax.axis_index(FAR), lax.axis_index(NEAR)
    peers = far * near
    own_rows = text_queries.shape[0]
    members = text_queries.shape[1] // HEAD_WIDTH
    lines = own_rows * members
    kv_rows = vision_keys.shape[0]
    features = vision.shape[1]
    near_id = my_near.reshape(1).astype(jnp.int32)

    own_text = jnp.stack(
        (text_queries.reshape(lines, HEAD_WIDTH), text_grads.reshape(lines, HEAD_WIDTH))
    )
    own_text = jnp.broadcast_to(own_text[None], (far, *own_text.shape))
    own_text, vision_keys, video_value_rows = lax.optimization_barrier(
        (own_text, vision_keys, video_value_rows)
    )
    text = lax.all_to_all(own_text, FAR, 0, 0, tiled=True)
    own_kv = jnp.stack((vision_keys, video_value_rows))
    all_kv = [own_kv] + [shifted(own_kv, NEAR, k) for k in range(1, near)]
    all_text = [text] + [shifted(text, NEAR, k) for k in range(1, near)]

    line_ids = jnp.arange(far * lines, dtype=jnp.int32)
    sources = jnp.stack(bases_from(my_near, near))
    row_of = (
        (line_ids // lines)[None, :] * (near * own_rows)
        + sources[:, None] * own_rows
        + (line_ids % lines // members)[None, :]
    )
    begin, end = row_bounds(lengths, frame_range, row_of.reshape(-1))
    steps = jnp.arange(FRAME_DEV, dtype=jnp.int32)
    first = (my_far * near + sources) * FRAME_DEV
    group_frames = (first[:, None] + steps[None, :]).reshape(-1)
    own_off = offsets(begin[: far * lines], end[: far * lines], group_frames)
    all_off = offsets(begin, end, first[0] + steps)
    chunks = far * lines // CHUNK
    all_off = all_off.reshape(near, chunks, FRAME_DEV, CHUNK)

    part = features // peers
    turned = pl.pallas_call(
        turn_kernel,
        out_shape=jax.ShapeDtypeStruct((near, far, part, kv_rows), BF16),
        grid=(far // 4,),
        in_specs=[SCALARS, pl.BlockSpec((kv_rows, 4 * near * part), lambda i: (0, i))],
        out_specs=pl.BlockSpec((near, 4, part, kv_rows), lambda i: (0, i, 0, 0)),
        compiler_params=LARGER,
    )(near_id, vision)
    turned = turned.reshape(near, far * part, kv_rows)
    text, turned = lax.optimization_barrier((text, turned))

    stats = pl.pallas_call(
        stats_kernel,
        out_shape=jax.ShapeDtypeStruct((far, 3 * chunks, CHUNK), F32),
        in_specs=[WHOLE] * (2 + near),
        out_specs=WHOLE,
        scratch_shapes=[pltpu.VMEM((3 * chunks, CHUNK), F32)],
        compiler_params=PARAMS,
    )(text, own_off, *all_kv)
    stats = lax.all_to_all(stats, FAR, 0, 0, tiled=True)
    norms = pl.pallas_call(
        join_kernel,
        out_shape=jax.ShapeDtypeStruct((near, 2 * chunks, CHUNK), F32),
        in_specs=[WHOLE],
        out_specs=WHOLE,
        compiler_params=PARAMS,
    )(stats)
    all_norm = lax.all_to_all(norms, NEAR, 0, 0, tiled=True)

    dq = pl.pallas_call(
        query_kernel,
        out_shape=jax.ShapeDtypeStruct((far, lines, HEAD_WIDTH), BF16),
        in_specs=[WHOLE] * (3 + near),
        out_specs=WHOLE,
        scratch_shapes=[pltpu.VMEM((kv_rows, CHUNK), BF16)],
        compiler_params=PARAMS,
    )(text, own_off, norms, *all_kv)
    dq, all_norm = lax.optimization_barrier((dq, all_norm))

    sums = pl.pallas_call(
        token_kernel,
        out_shape=[jax.ShapeDtypeStruct((far * part, 2 * HEAD_WIDTH), BF16)] * near,
        in_specs=[SCALARS] + [WHOLE] * 3 + [pl.BlockSpec(memory_space=pltpu.HBM)] + [WHOLE] * near,
        out_specs=[WHOLE] * near,
        scratch_shapes=[
            pltpu.VMEM((kv_rows, CHUNK), BF16),
            pltpu.VMEM((kv_rows, CHUNK), BF16),
            pltpu.VMEM((kv_rows, 2 * HEAD_WIDTH), BF16),
            pltpu.VMEM((near, far * part, kv_rows), BF16),
            pltpu.SemaphoreType.DMA((near,)),
        ],
        compiler_params=LARGE,
        cost_estimate=HEAVY,
    )(near_id, own_kv, all_off, all_norm, turned, *all_text)

    sums, dq = lax.optimization_barrier((sums, dq))
    dq = lax.all_to_all(dq, FAR, 0, 0, tiled=True)
    got = [sums[0]] + [shifted(sums[k], NEAR, k) for k in range(1, near)]

    dq = pl.pallas_call(
        sum_kernel,
        out_shape=jax.ShapeDtypeStruct((lines, HEAD_WIDTH), BF16),
        in_specs=[WHOLE],
        out_specs=WHOLE,
        compiler_params=PARAMS,
        cost_estimate=HEAVY,
    )(dq)
    dq = from_everyone(dq.reshape(own_rows, -1), FAR).reshape(far, own_rows, -1)

    weights = sum(one.astype(F32) for one in got).astype(BF16)
    weights, dq = lax.optimization_barrier((weights, dq))
    weights = lax.all_to_all(
        weights.reshape(far, part, 2 * HEAD_WIDTH), FAR, 0, 0, tiled=True
    )
    all_dq = [dq] + [shifted(dq, NEAR, k) for k in range(1, near)]
    query_grad = jnp.stack([lax.select_n(base, *all_dq) for base in bases_from(my_near, near)], 1)
    query_grad = query_grad.reshape(peers * own_rows, -1)
    weights = jnp.sum(weights.astype(F32), axis=0)
    return query_grad, weights[:, :HEAD_WIDTH], weights[:, HEAD_WIDTH:]


def solution(mesh):
    finer = Mesh(
        mesh.devices.reshape(2, 8, 4, mesh.shape["head"]), ("tok_0", "tok_1", "tok_2", "head")
    )
    return jax.shard_map(
        shards,
        mesh=finer,
        in_specs=(
            P(TOK, "head"),
            P(TOK, "head"),
            P(TOK, "head"),
            P(TOK, "head"),
            P(TOK, None),
            P(),
            P(),
        ),
        out_specs=(P(None, "head"), P(TOK, "head"), P(TOK, "head")),
        check_vma=False,
    )
```

```python
import jax
import jax.numpy as jnp
from jax import lax
from jax.experimental import pallas as pl
from jax.experimental.pallas import tpu as pltpu
from jax.sharding import Mesh
from jax.sharding import PartitionSpec as P

HEAD_WIDTH = 128
FRAME_DEV = 4
TOK = ("tok_0", "tok_1", "tok_2")
FAR = ("tok_0", "tok_1")
NEAR = "tok_2"
CHUNK = 256
SCALE = HEAD_WIDTH**-0.5
LOG2E = 1.4426950408889634
OFF = 1e30
LOW = -1e29
F32 = jnp.float32
BF16 = jnp.bfloat16
NT = (((1,), (1,)), ((), ()))
NN = (((1,), (0,)), ((), ()))
PARAMS = pltpu.CompilerParams(vmem_limit_bytes=32 * 2**20)
LARGE = pltpu.CompilerParams(vmem_limit_bytes=52 * 2**20)
LARGER = pltpu.CompilerParams(vmem_limit_bytes=58 * 2**20)
HEAVY = pl.CostEstimate(flops=10**11, bytes_accessed=2**20, transcendentals=0)
WHOLE = pl.BlockSpec(memory_space=pltpu.VMEM)
SCALARS = pl.BlockSpec(memory_space=pltpu.SMEM)


def from_everyone(x, axis):
    peers = lax.axis_size(axis)
    return lax.all_to_all(jnp.broadcast_to(x[None], (peers, *x.shape)), axis, 0, 0, tiled=True)


def shifted(x, axis, step):
    peers = lax.axis_size(axis)
    return lax.ppermute(x, axis, [(i, (i + step) % peers) for i in range(peers)])


def from_ring(xs, axis):
    peers = lax.axis_size(axis)
    order = sorted(range(1, peers), key=lambda k: -min(k, peers - k))
    got = {k: shifted(xs[k], axis, k) for k in order}
    return [xs[0]] + [got[k] for k in range(1, peers)]


def dot(a, b, dims):
    return lax.dot_general(a, b, dims, preferred_element_type=F32)


def chunk_of(text_ref, c, which):
    per = CHUNK // text_ref.shape[2]
    return text_ref[c * per : (c + 1) * per, which].reshape(CHUNK, HEAD_WIDTH)


def frame_slices(off_ref, c, rows, frames):
    for f in range(frames):
        yield slice(f * rows, (f + 1) * rows), off_ref[c, f : f + 1, :]


def join(parts):
    top = parts[0][0]
    for part in parts[1:]:
        top = jnp.maximum(top, part[0])
    total = jnp.zeros_like(top)
    weighted = jnp.zeros_like(top)
    for part in parts:
        factor = jnp.exp2(part[0] - top)
        total += part[1] * factor
        weighted += part[2] * factor
    return top, total, weighted


def piece_stats(q_c, g_c, kv_ref, off_ref, c):
    rows = kv_ref.shape[1] // FRAME_DEV
    scores = dot(kv_ref[0], q_c, NT) * (SCALE * LOG2E)
    dprobs = dot(kv_ref[1], g_c, NT)
    top = jnp.full((1, CHUNK), LOW, F32)
    for here, off in frame_slices(off_ref, c, rows, FRAME_DEV):
        top = jnp.maximum(top, jnp.max(scores[here], axis=0, keepdims=True) - off)
    total = jnp.zeros((1, CHUNK), F32)
    weighted = jnp.zeros((1, CHUNK), F32)
    for here, off in frame_slices(off_ref, c, rows, FRAME_DEV):
        terms = jnp.exp2(scores[here] - (top + off))
        total += jnp.sum(terms, axis=0, keepdims=True)
        weighted += jnp.sum(terms * dprobs[here], axis=0, keepdims=True)
    return top, total, weighted


def stats_kernel(text_ref, off_ref, *refs):
    kv_refs, all_ref, stats_scr = refs[:-2], refs[-2], refs[-1]
    chunks = stats_scr.shape[0] // 3
    for c in range(chunks):
        q_c, g_c = chunk_of(text_ref, c, 0), chunk_of(text_ref, c, 1)
        parts = []
        for p, kv_ref in enumerate(kv_refs):
            offs = off_ref.at[:, p * FRAME_DEV : (p + 1) * FRAME_DEV]
            parts.append(piece_stats(q_c, g_c, kv_ref, offs, c))
        for k, part in enumerate(join(parts)):
            stats_scr[k * chunks + c : k * chunks + c + 1, :] = part
    stats = stats_scr[...]
    for k in range(all_ref.shape[0]):
        all_ref[k] = stats


def join_kernel(stats_ref, out_ref):
    lines = stats_ref.shape[1] // 3
    parts = [
        [stats_ref[k, j * lines : (j + 1) * lines] for j in range(3)]
        for k in range(stats_ref.shape[0])
    ]
    top, total, weighted = join(parts)
    norm = jnp.concatenate((top + jnp.log2(total), weighted / total), axis=0)
    for k in range(out_ref.shape[0]):
        out_ref[k] = norm


def query_kernel(text_ref, off_ref, copies_ref, *refs):
    kv_refs, dq_ref, ds_scr = refs[:-2], refs[-2], refs[-1]
    norm_ref = copies_ref.at[0]
    chunks = norm_ref.shape[0] // 2
    per = CHUNK // dq_ref.shape[1]
    for c in range(chunks):
        q_c, g_c = chunk_of(text_ref, c, 0), chunk_of(text_ref, c, 1)
        shift = norm_ref[c : c + 1, :]
        delta = norm_ref[chunks + c : chunks + c + 1, :]
        dq = jnp.zeros((HEAD_WIDTH, CHUNK), F32)
        for p, kv_ref in enumerate(kv_refs):
            rows = kv_ref.shape[1] // FRAME_DEV
            scores = dot(kv_ref[0], q_c, NT) * (SCALE * LOG2E)
            dprobs = dot(kv_ref[1], g_c, NT)
            offs = off_ref.at[:, p * FRAME_DEV : (p + 1) * FRAME_DEV]
            for here, off in frame_slices(offs, c, rows, FRAME_DEV):
                probs = jnp.exp2(scores[here] - (shift + off))
                ds_scr[here] = (probs * (dprobs[here] - delta)).astype(BF16)
            dq += dot(kv_ref[0].T, ds_scr[...], NN)
        dq_ref[c * per : (c + 1) * per] = (dq * SCALE).T.reshape(per, dq_ref.shape[1], HEAD_WIDTH)


def token_kernel(near_ref, kv_ref, off_ref, norm_ref, far_vision_ref, *refs):
    pieces = off_ref.shape[0]
    text_refs, out_refs = refs[:pieces], refs[pieces : 2 * pieces]
    p_scr, ds_scr, kv_scr, vision_ref, vision_sem = refs[2 * pieces :]
    copies = [
        pltpu.make_async_copy(far_vision_ref.at[p], vision_ref.at[p], vision_sem.at[p])
        for p in range(pieces)
    ]
    for copy in copies:
        copy.start()
    chunks = norm_ref.shape[1] // 2
    rows = kv_ref.shape[1] // FRAME_DEV
    key_sum = jnp.zeros(kv_ref.shape[1:], F32)
    value_sum = jnp.zeros(kv_ref.shape[1:], F32)
    for p, text_ref in enumerate(text_refs):
        norm = norm_ref[(near_ref[0] + (pieces - p)) % pieces]
        for c in range(chunks):
            q_c, g_c = chunk_of(text_ref, c, 0), chunk_of(text_ref, c, 1)
            shift, delta = norm[c : c + 1], norm[chunks + c : chunks + c + 1]
            scores = dot(kv_ref[0], q_c, NT) * (SCALE * LOG2E)
            dprobs = dot(kv_ref[1], g_c, NT)
            for here, off in frame_slices(off_ref.at[p], c, rows, FRAME_DEV):
                probs = jnp.exp2(scores[here] - (shift + off))
                p_scr[here] = probs.astype(BF16)
                ds_scr[here] = (probs * (dprobs[here] - delta)).astype(BF16)
            value_sum += dot(p_scr[...], g_c, NN)
            key_sum += dot(ds_scr[...], q_c, NN)
    kv_scr[:, :HEAD_WIDTH] = (key_sum * SCALE).astype(BF16)
    kv_scr[:, HEAD_WIDTH:] = value_sum.astype(BF16)
    size = 512
    for p, out_ref in enumerate(out_refs):
        copies[p].wait()
        for at in range(0, out_ref.shape[0], size):
            block = vision_ref[p, at : at + size]
            out_ref[at : at + size] = dot(block, kv_scr[...], NN).astype(BF16)


def sum_kernel(parts_ref, out_ref):
    out_ref[...] = jnp.sum(parts_ref[...], axis=0).astype(BF16)


def total_kernel(parts_ref, key_ref, value_ref):
    total = jnp.sum(parts_ref[...].astype(F32), axis=0)
    key_ref[...] = total[:, :HEAD_WIDTH]
    value_ref[...] = total[:, HEAD_WIDTH:]


def turn_kernel(near_ref, vision_ref, out_ref):
    pieces, deep, size, _ = out_ref.shape
    for d in range(deep):
        turned = vision_ref[:, d * pieces * size : (d + 1) * pieces * size].T
        for p in range(pieces):
            at = lax.rem(p + pieces - near_ref[0], pieces)
            out_ref[at, d] = turned[p * size : (p + 1) * size]


def bases_from(at, peers):
    return [lax.rem(at + peers - k, jnp.int32(peers)) for k in range(peers)]


def row_bounds(lengths, frame_range, rows):
    part_ids = jnp.arange(lengths.shape[0], dtype=jnp.int32)
    ends = jnp.sum(jnp.where(part_ids[None, :] <= part_ids[:, None], lengths[None, :], 0), axis=1)
    segment = jnp.sum((rows[:, None] >= ends[None, :]).astype(jnp.int32), axis=1)
    pick = (segment[:, None] == part_ids[None, :]).astype(jnp.int32)
    begin = jnp.sum(pick * frame_range[None, :, 0], axis=1)
    end = jnp.sum(pick * frame_range[None, :, 1], axis=1)
    return begin, end


def offsets(begin, end, at):
    allowed = (at[:, None] >= begin[None, :]) & (at[:, None] < end[None, :])
    off = jnp.where(allowed, 0.0, OFF).astype(F32)
    return off.reshape(at.shape[0], -1, CHUNK).transpose(1, 0, 2)


def shards(text_queries, text_grads, vision_keys, video_value_rows, vision, lengths, frame_range):
    far, near = lax.axis_size(FAR), lax.axis_size(NEAR)
    my_far, my_near = lax.axis_index(FAR), lax.axis_index(NEAR)
    peers = far * near
    own_rows = text_queries.shape[0]
    members = text_queries.shape[1] // HEAD_WIDTH
    lines = own_rows * members
    kv_rows = vision_keys.shape[0]
    features = vision.shape[1]
    near_id = my_near.reshape(1).astype(jnp.int32)

    own_text = jnp.stack(
        (text_queries.reshape(lines, HEAD_WIDTH), text_grads.reshape(lines, HEAD_WIDTH))
    )
    own_text = jnp.broadcast_to(own_text[None], (far, *own_text.shape))
    own_text, vision_keys, video_value_rows = lax.optimization_barrier(
        (own_text, vision_keys, video_value_rows)
    )
    text = lax.all_to_all(own_text, FAR, 0, 0, tiled=True)
    own_kv = jnp.stack((vision_keys, video_value_rows))
    all_kv = from_ring([own_kv] * near, NEAR)
    all_text = from_ring([text] * near, NEAR)

    line_ids = jnp.arange(far * lines, dtype=jnp.int32)
    sources = jnp.stack(bases_from(my_near, near))
    row_of = (
        (line_ids // lines)[None, :] * (near * own_rows)
        + sources[:, None] * own_rows
        + (line_ids % lines // members)[None, :]
    )
    begin, end = row_bounds(lengths, frame_range, row_of.reshape(-1))
    steps = jnp.arange(FRAME_DEV, dtype=jnp.int32)
    first = (my_far * near + sources) * FRAME_DEV
    group_frames = (first[:, None] + steps[None, :]).reshape(-1)
    own_off = offsets(begin[: far * lines], end[: far * lines], group_frames)
    all_off = offsets(begin, end, first[0] + steps)
    chunks = far * lines // CHUNK
    all_off = all_off.reshape(near, chunks, FRAME_DEV, CHUNK)

    part = features // peers
    turned = pl.pallas_call(
        turn_kernel,
        out_shape=jax.ShapeDtypeStruct((near, far, part, kv_rows), BF16),
        grid=(far // 4,),
        in_specs=[SCALARS, pl.BlockSpec((kv_rows, 4 * near * part), lambda i: (0, i))],
        out_specs=pl.BlockSpec((near, 4, part, kv_rows), lambda i: (0, i, 0, 0)),
        compiler_params=LARGER,
    )(near_id, vision)
    turned = turned.reshape(near, far * part, kv_rows)
    text, turned = lax.optimization_barrier((text, turned))

    stats = pl.pallas_call(
        stats_kernel,
        out_shape=jax.ShapeDtypeStruct((far, 3 * chunks, CHUNK), F32),
        in_specs=[WHOLE] * (2 + near),
        out_specs=WHOLE,
        scratch_shapes=[pltpu.VMEM((3 * chunks, CHUNK), F32)],
        compiler_params=PARAMS,
    )(text, own_off, *all_kv)
    stats = lax.all_to_all(stats, FAR, 0, 0, tiled=True)
    norms = pl.pallas_call(
        join_kernel,
        out_shape=jax.ShapeDtypeStruct((near, 2 * chunks, CHUNK), F32),
        in_specs=[WHOLE],
        out_specs=WHOLE,
        compiler_params=PARAMS,
    )(stats)
    all_norm = lax.all_to_all(norms, NEAR, 0, 0, tiled=True)

    dq = pl.pallas_call(
        query_kernel,
        out_shape=jax.ShapeDtypeStruct((far, lines, HEAD_WIDTH), F32),
        in_specs=[WHOLE] * (3 + near),
        out_specs=WHOLE,
        scratch_shapes=[pltpu.VMEM((kv_rows, CHUNK), BF16)],
        compiler_params=PARAMS,
    )(text, own_off, norms, *all_kv)
    dq, all_norm = lax.optimization_barrier((dq, all_norm))
    dq = lax.all_to_all(dq, FAR, 0, 0, tiled=True)

    sums = pl.pallas_call(
        token_kernel,
        out_shape=[jax.ShapeDtypeStruct((far * part, 2 * HEAD_WIDTH), BF16)] * near,
        in_specs=[SCALARS] + [WHOLE] * 3 + [pl.BlockSpec(memory_space=pltpu.HBM)] + [WHOLE] * near,
        out_specs=[WHOLE] * near,
        scratch_shapes=[
            pltpu.VMEM((kv_rows, CHUNK), BF16),
            pltpu.VMEM((kv_rows, CHUNK), BF16),
            pltpu.VMEM((kv_rows, 2 * HEAD_WIDTH), BF16),
            pltpu.VMEM((near, far * part, kv_rows), BF16),
            pltpu.SemaphoreType.DMA((near,)),
        ],
        compiler_params=LARGE,
        cost_estimate=HEAVY,
    )(near_id, own_kv, all_off, all_norm, turned, *all_text)

    got = from_ring(sums, NEAR)

    dq = pl.pallas_call(
        sum_kernel,
        out_shape=jax.ShapeDtypeStruct((lines, HEAD_WIDTH), BF16),
        in_specs=[WHOLE],
        out_specs=WHOLE,
        compiler_params=PARAMS,
        cost_estimate=HEAVY,
    )(dq)
    dq = from_everyone(dq.reshape(own_rows, -1), FAR).reshape(far, own_rows, -1)

    weights = sum(one.astype(F32) for one in got).astype(BF16)
    weights, dq = lax.optimization_barrier((weights, dq))
    weights = lax.all_to_all(
        weights.reshape(far, part, 2 * HEAD_WIDTH), FAR, 0, 0, tiled=True
    )
    all_dq = from_ring([dq] * near, NEAR)
    query_grad = jnp.stack([lax.select_n(base, *all_dq) for base in bases_from(my_near, near)], 1)
    query_grad = query_grad.reshape(peers * own_rows, -1)
    key_weights, value_weights = pl.pallas_call(
        total_kernel,
        out_shape=[jax.ShapeDtypeStruct((part, HEAD_WIDTH), F32)] * 2,
        in_specs=[WHOLE],
        out_specs=[WHOLE] * 2,
        compiler_params=PARAMS,
    )(weights)
    return query_grad, key_weights, value_weights


def solution(mesh):
    finer = Mesh(
        mesh.devices.reshape(2, 8, 4, mesh.shape["head"]), ("tok_0", "tok_1", "tok_2", "head")
    )
    return jax.shard_map(
        shards,
        mesh=finer,
        in_specs=(
            P(TOK, "head"),
            P(TOK, "head"),
            P(TOK, "head"),
            P(TOK, "head"),
            P(TOK, None),
            P(),
            P(),
        ),
        out_specs=(P(None, "head"), P(TOK, "head"), P(TOK, "head")),
        check_vma=False,
    )
```

```python
import jax
import jax.numpy as jnp
from jax import lax
from jax.experimental import pallas as pl
from jax.experimental.pallas import tpu as pltpu
from jax.sharding import Mesh
from jax.sharding import PartitionSpec as P

HEAD_WIDTH = 128
FRAME_DEV = 4
TOK = ("tok_0", "tok_1", "tok_2", "tok_3")
FAR = ("tok_0", "tok_1", "tok_2")
NEAR = "tok_3"
PLANE = ("tok_0", "tok_1")
LINE = ("tok_2", "tok_3")
CHUNK = 256
SCALE = HEAD_WIDTH**-0.5
LOG2E = 1.4426950408889634
OFF = 1e30
LOW = -1e29
F32 = jnp.float32
BF16 = jnp.bfloat16
NT = (((1,), (1,)), ((), ()))
NN = (((1,), (0,)), ((), ()))
PARAMS = pltpu.CompilerParams(vmem_limit_bytes=32 * 2**20)
LARGE = pltpu.CompilerParams(vmem_limit_bytes=49 * 2**20)
LARGER = pltpu.CompilerParams(vmem_limit_bytes=58 * 2**20)
HEAVY = pl.CostEstimate(flops=10**11, bytes_accessed=2**20, transcendentals=0)
WHOLE = pl.BlockSpec(memory_space=pltpu.VMEM)
SCALARS = pl.BlockSpec(memory_space=pltpu.SMEM)


def from_everyone(x, axis):
    peers = lax.axis_size(axis)
    return lax.all_to_all(jnp.broadcast_to(x[None], (peers, *x.shape)), axis, 0, 0, tiled=True)


def shifted(x, axis, step):
    peers = lax.axis_size(axis)
    return lax.ppermute(x, axis, [(i, (i + step) % peers) for i in range(peers)])


def from_ring(xs, axis):
    peers = lax.axis_size(axis)
    order = sorted(range(1, peers), key=lambda k: -min(k, peers - k))
    got = {k: shifted(xs[k], axis, k) for k in order}
    return [xs[0]] + [got[k] for k in range(1, peers)]


def dot(a, b, dims):
    return lax.dot_general(a, b, dims, preferred_element_type=F32)


def chunk_of(text_ref, c, which):
    per = CHUNK // text_ref.shape[2]
    return text_ref[c * per : (c + 1) * per, which].reshape(CHUNK, HEAD_WIDTH)


def frame_slices(off_ref, c, rows, frames):
    for f in range(frames):
        yield slice(f * rows, (f + 1) * rows), off_ref[c, f : f + 1, :]


def join(parts):
    top = parts[0][0]
    for part in parts[1:]:
        top = jnp.maximum(top, part[0])
    total = jnp.zeros_like(top)
    weighted = jnp.zeros_like(top)
    for part in parts:
        factor = jnp.exp2(part[0] - top)
        total += part[1] * factor
        weighted += part[2] * factor
    return top, total, weighted


def piece_stats(q_c, g_c, kv_ref, off_ref, c):
    rows = kv_ref.shape[1] // FRAME_DEV
    scores = dot(kv_ref[0], q_c, NT) * (SCALE * LOG2E)
    dprobs = dot(kv_ref[1], g_c, NT)
    top = jnp.full((1, CHUNK), LOW, F32)
    for here, off in frame_slices(off_ref, c, rows, FRAME_DEV):
        top = jnp.maximum(top, jnp.max(scores[here], axis=0, keepdims=True) - off)
    total = jnp.zeros((1, CHUNK), F32)
    weighted = jnp.zeros((1, CHUNK), F32)
    for here, off in frame_slices(off_ref, c, rows, FRAME_DEV):
        terms = jnp.exp2(scores[here] - (top + off))
        total += jnp.sum(terms, axis=0, keepdims=True)
        weighted += jnp.sum(terms * dprobs[here], axis=0, keepdims=True)
    return top, total, weighted


def stats_kernel(text_ref, off_ref, *refs):
    kv_refs, all_ref, stats_scr = refs[:-2], refs[-2], refs[-1]
    chunks = stats_scr.shape[0] // 3
    for c in range(chunks):
        q_c, g_c = chunk_of(text_ref, c, 0), chunk_of(text_ref, c, 1)
        parts = []
        for p, kv_ref in enumerate(kv_refs):
            offs = off_ref.at[:, p * FRAME_DEV : (p + 1) * FRAME_DEV]
            parts.append(piece_stats(q_c, g_c, kv_ref, offs, c))
        for k, part in enumerate(join(parts)):
            stats_scr[k * chunks + c : k * chunks + c + 1, :] = part
    stats = stats_scr[...]
    for k in range(all_ref.shape[0]):
        all_ref[k] = stats


def join_kernel(stats_ref, out_ref):
    lines = stats_ref.shape[1] // 3
    parts = [
        [stats_ref[k, j * lines : (j + 1) * lines] for j in range(3)]
        for k in range(stats_ref.shape[0])
    ]
    top, total, weighted = join(parts)
    norm = jnp.concatenate((top + jnp.log2(total), weighted / total), axis=0)
    for k in range(out_ref.shape[0]):
        out_ref[k] = norm


def query_kernel(text_ref, off_ref, copies_ref, *refs):
    kv_refs, dq_ref, ds_scr = refs[:-2], refs[-2], refs[-1]
    norm_ref = copies_ref.at[0]
    chunks = norm_ref.shape[0] // 2
    per = CHUNK // dq_ref.shape[1]
    for c in range(chunks):
        q_c, g_c = chunk_of(text_ref, c, 0), chunk_of(text_ref, c, 1)
        shift = norm_ref[c : c + 1, :]
        delta = norm_ref[chunks + c : chunks + c + 1, :]
        dq = jnp.zeros((HEAD_WIDTH, CHUNK), F32)
        for p, kv_ref in enumerate(kv_refs):
            rows = kv_ref.shape[1] // FRAME_DEV
            scores = dot(kv_ref[0], q_c, NT) * (SCALE * LOG2E)
            dprobs = dot(kv_ref[1], g_c, NT)
            offs = off_ref.at[:, p * FRAME_DEV : (p + 1) * FRAME_DEV]
            for here, off in frame_slices(offs, c, rows, FRAME_DEV):
                probs = jnp.exp2(scores[here] - (shift + off))
                ds_scr[here] = (probs * (dprobs[here] - delta)).astype(BF16)
            dq += dot(kv_ref[0].T, ds_scr[...], NN)
        dq_ref[c * per : (c + 1) * per] = (dq * SCALE).T.reshape(per, dq_ref.shape[1], HEAD_WIDTH)


def token_kernel(near_ref, kv_ref, off_ref, norm_ref, far_vision_ref, *refs):
    pieces = off_ref.shape[0]
    out_count = far_vision_ref.shape[0]
    text_refs, refs = refs[:pieces], refs[pieces:]
    out_refs = refs[:out_count]
    p_scr, ds_scr, kv_scr, vision_ref, vision_sem = refs[out_count:]
    copies = [
        pltpu.make_async_copy(far_vision_ref.at[p], vision_ref.at[p], vision_sem.at[p])
        for p in range(out_count)
    ]
    for copy in copies:
        copy.start()
    chunks = norm_ref.shape[1] // 2
    rows = kv_ref.shape[1] // FRAME_DEV
    key_sum = jnp.zeros(kv_ref.shape[1:], F32)
    value_sum = jnp.zeros(kv_ref.shape[1:], F32)
    for p, text_ref in enumerate(text_refs):
        norm = norm_ref[(near_ref[0] + (pieces - p)) % pieces]
        for c in range(chunks):
            q_c, g_c = chunk_of(text_ref, c, 0), chunk_of(text_ref, c, 1)
            shift, delta = norm[c : c + 1], norm[chunks + c : chunks + c + 1]
            scores = dot(kv_ref[0], q_c, NT) * (SCALE * LOG2E)
            dprobs = dot(kv_ref[1], g_c, NT)
            for here, off in frame_slices(off_ref.at[p], c, rows, FRAME_DEV):
                probs = jnp.exp2(scores[here] - (shift + off))
                p_scr[here] = probs.astype(BF16)
                ds_scr[here] = (probs * (dprobs[here] - delta)).astype(BF16)
            value_sum += dot(p_scr[...], g_c, NN)
            key_sum += dot(ds_scr[...], q_c, NN)
    kv_scr[:, :HEAD_WIDTH] = (key_sum * SCALE).astype(BF16)
    kv_scr[:, HEAD_WIDTH:] = value_sum.astype(BF16)
    size = 512
    for p, out_ref in enumerate(out_refs):
        copies[p].wait()
        for at in range(0, out_ref.shape[0], size):
            block = vision_ref[p, at : at + size]
            out_ref[at : at + size] = dot(block, kv_scr[...], NN).astype(BF16)


def sum_kernel(parts_ref, out_ref):
    out_ref[...] = jnp.sum(parts_ref[...], axis=0).astype(BF16)


def total_kernel(parts_ref, key_ref, value_ref):
    total = jnp.sum(parts_ref[...].astype(F32), axis=0)
    key_ref[...] = total[:, :HEAD_WIDTH]
    value_ref[...] = total[:, HEAD_WIDTH:]


def turn_kernel(near_ref, vision_ref, out_ref):
    pieces, deep, size, _ = out_ref.shape
    for d in range(deep):
        turned = vision_ref[:, d * pieces * size : (d + 1) * pieces * size].T
        for p in range(pieces):
            at = lax.rem(p + pieces - near_ref[0], pieces)
            out_ref[at, d] = turned[p * size : (p + 1) * size]


def bases_from(at, peers):
    return [lax.rem(at + peers - k, jnp.int32(peers)) for k in range(peers)]


def row_bounds(lengths, frame_range, rows):
    part_ids = jnp.arange(lengths.shape[0], dtype=jnp.int32)
    ends = jnp.sum(jnp.where(part_ids[None, :] <= part_ids[:, None], lengths[None, :], 0), axis=1)
    segment = jnp.sum((rows[:, None] >= ends[None, :]).astype(jnp.int32), axis=1)
    pick = (segment[:, None] == part_ids[None, :]).astype(jnp.int32)
    begin = jnp.sum(pick * frame_range[None, :, 0], axis=1)
    end = jnp.sum(pick * frame_range[None, :, 1], axis=1)
    return begin, end


def offsets(begin, end, at):
    allowed = (at[:, None] >= begin[None, :]) & (at[:, None] < end[None, :])
    off = jnp.where(allowed, 0.0, OFF).astype(F32)
    return off.reshape(at.shape[0], -1, CHUNK).transpose(1, 0, 2)


def shards(text_queries, text_grads, vision_keys, video_value_rows, vision, lengths, frame_range):
    far, near = lax.axis_size(FAR), lax.axis_size(NEAR)
    my_far, my_near = lax.axis_index(FAR), lax.axis_index(NEAR)
    peers = far * near
    own_rows = text_queries.shape[0]
    members = text_queries.shape[1] // HEAD_WIDTH
    lines = own_rows * members
    kv_rows = vision_keys.shape[0]
    features = vision.shape[1]
    plane, line = lax.axis_size(PLANE), lax.axis_size(LINE)
    line_id = lax.axis_index(LINE).reshape(1).astype(jnp.int32)
    near_id = my_near.reshape(1).astype(jnp.int32)

    own_text = jnp.stack(
        (text_queries.reshape(lines, HEAD_WIDTH), text_grads.reshape(lines, HEAD_WIDTH))
    )
    own_text = jnp.broadcast_to(own_text[None], (far, *own_text.shape))
    own_text, vision_keys, video_value_rows = lax.optimization_barrier(
        (own_text, vision_keys, video_value_rows)
    )
    text = lax.all_to_all(own_text, FAR, 0, 0, tiled=True)
    own_kv = jnp.stack((vision_keys, video_value_rows))
    all_kv = from_ring([own_kv] * near, NEAR)
    all_text = from_ring([text] * near, NEAR)

    line_ids = jnp.arange(far * lines, dtype=jnp.int32)
    sources = jnp.stack(bases_from(my_near, near))
    row_of = (
        (line_ids // lines)[None, :] * (near * own_rows)
        + sources[:, None] * own_rows
        + (line_ids % lines // members)[None, :]
    )
    begin, end = row_bounds(lengths, frame_range, row_of.reshape(-1))
    steps = jnp.arange(FRAME_DEV, dtype=jnp.int32)
    first = (my_far * near + sources) * FRAME_DEV
    group_frames = (first[:, None] + steps[None, :]).reshape(-1)
    own_off = offsets(begin[: far * lines], end[: far * lines], group_frames)
    all_off = offsets(begin, end, first[0] + steps)
    chunks = far * lines // CHUNK
    all_off = all_off.reshape(near, chunks, FRAME_DEV, CHUNK)

    part = features // peers
    turned = pl.pallas_call(
        turn_kernel,
        out_shape=jax.ShapeDtypeStruct((line, plane, part, kv_rows), BF16),
        grid=(plane // 4,),
        in_specs=[SCALARS, pl.BlockSpec((kv_rows, 4 * line * part), lambda i: (0, i))],
        out_specs=pl.BlockSpec((line, 4, part, kv_rows), lambda i: (0, i, 0, 0)),
        compiler_params=LARGER,
    )(line_id, vision)
    turned = turned.reshape(line, plane * part, kv_rows)
    text, turned = lax.optimization_barrier((text, turned))

    stats = pl.pallas_call(
        stats_kernel,
        out_shape=jax.ShapeDtypeStruct((far, 3 * chunks, CHUNK), F32),
        in_specs=[WHOLE] * (2 + near),
        out_specs=WHOLE,
        scratch_shapes=[pltpu.VMEM((3 * chunks, CHUNK), F32)],
        compiler_params=PARAMS,
    )(text, own_off, *all_kv)
    stats = lax.all_to_all(stats, FAR, 0, 0, tiled=True)
    norms = pl.pallas_call(
        join_kernel,
        out_shape=jax.ShapeDtypeStruct((near, 2 * chunks, CHUNK), F32),
        in_specs=[WHOLE],
        out_specs=WHOLE,
        compiler_params=PARAMS,
    )(stats)
    all_norm = lax.all_to_all(norms, NEAR, 0, 0, tiled=True)

    dq = pl.pallas_call(
        query_kernel,
        out_shape=jax.ShapeDtypeStruct((far, lines, HEAD_WIDTH), F32),
        in_specs=[WHOLE] * (3 + near),
        out_specs=WHOLE,
        scratch_shapes=[pltpu.VMEM((kv_rows, CHUNK), BF16)],
        compiler_params=PARAMS,
    )(text, own_off, norms, *all_kv)
    dq, all_norm = lax.optimization_barrier((dq, all_norm))
    dq = lax.all_to_all(dq, FAR, 0, 0, tiled=True)

    sums = pl.pallas_call(
        token_kernel,
        out_shape=[jax.ShapeDtypeStruct((plane * part, 2 * HEAD_WIDTH), BF16)] * line,
        in_specs=[SCALARS] + [WHOLE] * 3 + [pl.BlockSpec(memory_space=pltpu.HBM)] + [WHOLE] * near,
        out_specs=[WHOLE] * line,
        scratch_shapes=[
            pltpu.VMEM((kv_rows, CHUNK), BF16),
            pltpu.VMEM((kv_rows, CHUNK), BF16),
            pltpu.VMEM((kv_rows, 2 * HEAD_WIDTH), BF16),
            pltpu.VMEM((line, plane * part, kv_rows), BF16),
            pltpu.SemaphoreType.DMA((line,)),
        ],
        compiler_params=LARGE,
        cost_estimate=HEAVY,
    )(near_id, own_kv, all_off, all_norm, turned, *all_text)

    got = from_ring(sums, LINE)

    dq = pl.pallas_call(
        sum_kernel,
        out_shape=jax.ShapeDtypeStruct((lines, HEAD_WIDTH), BF16),
        in_specs=[WHOLE],
        out_specs=WHOLE,
        compiler_params=PARAMS,
        cost_estimate=HEAVY,
    )(dq)
    dq = from_everyone(dq.reshape(own_rows, -1), FAR).reshape(far, own_rows, -1)

    weights = sum(one.astype(F32) for one in got).astype(BF16)
    weights, dq = lax.optimization_barrier((weights, dq))
    weights = lax.all_to_all(
        weights.reshape(plane, part, 2 * HEAD_WIDTH), PLANE, 0, 0, tiled=True
    )
    all_dq = from_ring([dq] * near, NEAR)
    query_grad = jnp.stack([lax.select_n(base, *all_dq) for base in bases_from(my_near, near)], 1)
    query_grad = query_grad.reshape(peers * own_rows, -1)
    key_weights, value_weights = pl.pallas_call(
        total_kernel,
        out_shape=[jax.ShapeDtypeStruct((part, HEAD_WIDTH), F32)] * 2,
        in_specs=[WHOLE],
        out_specs=[WHOLE] * 2,
        compiler_params=PARAMS,
    )(weights)
    return query_grad, key_weights, value_weights


def solution(mesh):
    finer = Mesh(
        mesh.devices.reshape(2, 8, 2, 2, mesh.shape["head"]),
        ("tok_0", "tok_1", "tok_2", "tok_3", "head"),
    )
    return jax.shard_map(
        shards,
        mesh=finer,
        in_specs=(
            P(TOK, "head"),
            P(TOK, "head"),
            P(TOK, "head"),
            P(TOK, "head"),
            P(TOK, None),
            P(),
            P(),
        ),
        out_specs=(P(None, "head"), P(TOK, "head"), P(TOK, "head")),
        check_vma=False,
    )
```

```python
import jax
import jax.numpy as jnp
from jax import lax
from jax.experimental import pallas as pl
from jax.experimental.pallas import tpu as pltpu
from jax.sharding import Mesh
from jax.sharding import PartitionSpec as P

HEAD_WIDTH = 128
FRAME_DEV = 4
TOK = ("tok_0", "tok_1", "tok_2")
FAR = ("tok_0", "tok_1")
NEAR = "tok_2"
CHUNK = 256
SCALE = HEAD_WIDTH**-0.5
LOG2E = 1.4426950408889634
OFF = 1e30
LOW = -1e29
F32 = jnp.float32
BF16 = jnp.bfloat16
NT = (((1,), (1,)), ((), ()))
NN = (((1,), (0,)), ((), ()))
PARAMS = pltpu.CompilerParams(vmem_limit_bytes=32 * 2**20)
LARGE = pltpu.CompilerParams(vmem_limit_bytes=52 * 2**20)
LARGER = pltpu.CompilerParams(vmem_limit_bytes=58 * 2**20)
HEAVY = pl.CostEstimate(flops=10**11, bytes_accessed=2**20, transcendentals=0)
WHOLE = pl.BlockSpec(memory_space=pltpu.VMEM)
SCALARS = pl.BlockSpec(memory_space=pltpu.SMEM)


def from_everyone(x, axis):
    peers = lax.axis_size(axis)
    return lax.all_to_all(jnp.broadcast_to(x[None], (peers, *x.shape)), axis, 0, 0, tiled=True)


def shifted(x, axis, step):
    peers = lax.axis_size(axis)
    return lax.ppermute(x, axis, [(i, (i + step) % peers) for i in range(peers)])


def from_ring(xs, axis):
    peers = lax.axis_size(axis)
    order = sorted(range(1, peers), key=lambda k: -min(k, peers - k))
    got = {k: shifted(xs[k], axis, k) for k in order}
    return [xs[0]] + [got[k] for k in range(1, peers)]


def dot(a, b, dims):
    return lax.dot_general(a, b, dims, preferred_element_type=F32)


def chunk_of(text_ref, c, which):
    per = CHUNK // text_ref.shape[2]
    return text_ref[c * per : (c + 1) * per, which].reshape(CHUNK, HEAD_WIDTH)


def frame_slices(off_ref, c, rows, frames):
    for f in range(frames):
        yield slice(f * rows, (f + 1) * rows), off_ref[c, f : f + 1, :]


def join(parts):
    top = parts[0][0]
    for part in parts[1:]:
        top = jnp.maximum(top, part[0])
    total = jnp.zeros_like(top)
    weighted = jnp.zeros_like(top)
    for part in parts:
        factor = jnp.exp2(part[0] - top)
        total += part[1] * factor
        weighted += part[2] * factor
    return top, total, weighted


def piece_stats(q_c, g_c, kv_ref, off_ref, c):
    rows = kv_ref.shape[1] // FRAME_DEV
    scores = dot(kv_ref[0], q_c, NT) * (SCALE * LOG2E)
    dprobs = dot(kv_ref[1], g_c, NT)
    top = jnp.full((1, CHUNK), LOW, F32)
    for here, off in frame_slices(off_ref, c, rows, FRAME_DEV):
        top = jnp.maximum(top, jnp.max(scores[here], axis=0, keepdims=True) - off)
    total = jnp.zeros((1, CHUNK), F32)
    weighted = jnp.zeros((1, CHUNK), F32)
    for here, off in frame_slices(off_ref, c, rows, FRAME_DEV):
        terms = jnp.exp2(scores[here] - (top + off))
        total += jnp.sum(terms, axis=0, keepdims=True)
        weighted += jnp.sum(terms * dprobs[here], axis=0, keepdims=True)
    return top, total, weighted


def stats_kernel(text_ref, off_ref, *refs):
    kv_refs, all_ref, stats_scr = refs[:-2], refs[-2], refs[-1]
    chunks = stats_scr.shape[0] // 3
    for c in range(chunks):
        q_c, g_c = chunk_of(text_ref, c, 0), chunk_of(text_ref, c, 1)
        parts = []
        for p, kv_ref in enumerate(kv_refs):
            offs = off_ref.at[:, p * FRAME_DEV : (p + 1) * FRAME_DEV]
            parts.append(piece_stats(q_c, g_c, kv_ref, offs, c))
        for k, part in enumerate(join(parts)):
            stats_scr[k * chunks + c : k * chunks + c + 1, :] = part
    stats = stats_scr[...]
    for k in range(all_ref.shape[0]):
        all_ref[k] = stats


def join_kernel(stats_ref, out_ref):
    lines = stats_ref.shape[1] // 3
    parts = [
        [stats_ref[k, j * lines : (j + 1) * lines] for j in range(3)]
        for k in range(stats_ref.shape[0])
    ]
    top, total, weighted = join(parts)
    norm = jnp.concatenate((top + jnp.log2(total), weighted / total), axis=0)
    for k in range(out_ref.shape[0]):
        out_ref[k] = norm


def query_kernel(text_ref, off_ref, copies_ref, *refs):
    kv_refs, dq_ref, ds_scr = refs[:-2], refs[-2], refs[-1]
    norm_ref = copies_ref.at[0]
    chunks = norm_ref.shape[0] // 2
    per = CHUNK // dq_ref.shape[1]
    for c in range(chunks):
        q_c, g_c = chunk_of(text_ref, c, 0), chunk_of(text_ref, c, 1)
        shift = norm_ref[c : c + 1, :]
        delta = norm_ref[chunks + c : chunks + c + 1, :]
        dq = jnp.zeros((HEAD_WIDTH, CHUNK), F32)
        for p, kv_ref in enumerate(kv_refs):
            rows = kv_ref.shape[1] // FRAME_DEV
            scores = dot(kv_ref[0], q_c, NT) * (SCALE * LOG2E)
            dprobs = dot(kv_ref[1], g_c, NT)
            offs = off_ref.at[:, p * FRAME_DEV : (p + 1) * FRAME_DEV]
            for here, off in frame_slices(offs, c, rows, FRAME_DEV):
                probs = jnp.exp2(scores[here] - (shift + off))
                ds_scr[here] = (probs * (dprobs[here] - delta)).astype(BF16)
            dq += dot(kv_ref[0].T, ds_scr[...], NN)
        dq_ref[c * per : (c + 1) * per] = (dq * SCALE).T.reshape(per, dq_ref.shape[1], HEAD_WIDTH)


def token_kernel(near_ref, kv_ref, off_ref, norm_ref, far_vision_ref, *refs):
    pieces = off_ref.shape[0]
    text_refs, out_refs = refs[:pieces], refs[pieces : 2 * pieces]
    p_scr, ds_scr, kv_scr, vision_ref, vision_sem = refs[2 * pieces :]
    copies = [
        pltpu.make_async_copy(far_vision_ref.at[p], vision_ref.at[p], vision_sem.at[p])
        for p in range(1, pieces)
    ]
    for copy in copies:
        copy.start()
    chunks = norm_ref.shape[1] // 2
    rows = kv_ref.shape[1] // FRAME_DEV
    key_sum = jnp.zeros(kv_ref.shape[1:], F32)
    value_sum = jnp.zeros(kv_ref.shape[1:], F32)
    for p, text_ref in enumerate(text_refs):
        norm = norm_ref[(near_ref[0] + (pieces - p)) % pieces]
        for c in range(chunks):
            q_c, g_c = chunk_of(text_ref, c, 0), chunk_of(text_ref, c, 1)
            shift, delta = norm[c : c + 1], norm[chunks + c : chunks + c + 1]
            scores = dot(kv_ref[0], q_c, NT) * (SCALE * LOG2E)
            dprobs = dot(kv_ref[1], g_c, NT)
            for here, off in frame_slices(off_ref.at[p], c, rows, FRAME_DEV):
                probs = jnp.exp2(scores[here] - (shift + off))
                p_scr[here] = probs.astype(BF16)
                ds_scr[here] = (probs * (dprobs[here] - delta)).astype(BF16)
            value_sum += dot(p_scr[...], g_c, NN)
            key_sum += dot(ds_scr[...], q_c, NN)
    kv_scr[:, :HEAD_WIDTH] = (key_sum * SCALE).astype(BF16)
    kv_scr[:, HEAD_WIDTH:] = value_sum.astype(BF16)
    size = 512
    out_refs[0][...] = kv_scr[...]
    for p, out_ref in list(enumerate(out_refs))[1:]:
        copies[p - 1].wait()
        for at in range(0, out_ref.shape[0], size):
            block = vision_ref[p, at : at + size]
            out_ref[at : at + size] = dot(block, kv_scr[...], NN).astype(BF16)


def own_kernel(vision_ref, kv_ref, out_ref):
    out_ref[...] = dot(vision_ref[0], kv_ref[...], NN).astype(BF16)


def sum_kernel(parts_ref, out_ref):
    out_ref[...] = jnp.sum(parts_ref[...], axis=0).astype(BF16)


def total_kernel(parts_ref, key_ref, value_ref):
    total = jnp.sum(parts_ref[...].astype(F32), axis=0)
    key_ref[...] = total[:, :HEAD_WIDTH]
    value_ref[...] = total[:, HEAD_WIDTH:]


def turn_kernel(near_ref, vision_ref, out_ref):
    pieces, deep, size, _ = out_ref.shape
    for d in range(deep):
        turned = vision_ref[:, d * pieces * size : (d + 1) * pieces * size].T
        for p in range(pieces):
            at = lax.rem(p + pieces - near_ref[0], pieces)
            out_ref[at, d] = turned[p * size : (p + 1) * size]


def bases_from(at, peers):
    return [lax.rem(at + peers - k, jnp.int32(peers)) for k in range(peers)]


def row_bounds(lengths, frame_range, rows):
    part_ids = jnp.arange(lengths.shape[0], dtype=jnp.int32)
    ends = jnp.sum(jnp.where(part_ids[None, :] <= part_ids[:, None], lengths[None, :], 0), axis=1)
    segment = jnp.sum((rows[:, None] >= ends[None, :]).astype(jnp.int32), axis=1)
    pick = (segment[:, None] == part_ids[None, :]).astype(jnp.int32)
    begin = jnp.sum(pick * frame_range[None, :, 0], axis=1)
    end = jnp.sum(pick * frame_range[None, :, 1], axis=1)
    return begin, end


def offsets(begin, end, at):
    allowed = (at[:, None] >= begin[None, :]) & (at[:, None] < end[None, :])
    off = jnp.where(allowed, 0.0, OFF).astype(F32)
    return off.reshape(at.shape[0], -1, CHUNK).transpose(1, 0, 2)


def shards(text_queries, text_grads, vision_keys, video_value_rows, vision, lengths, frame_range):
    far, near = lax.axis_size(FAR), lax.axis_size(NEAR)
    my_far, my_near = lax.axis_index(FAR), lax.axis_index(NEAR)
    peers = far * near
    own_rows = text_queries.shape[0]
    members = text_queries.shape[1] // HEAD_WIDTH
    lines = own_rows * members
    kv_rows = vision_keys.shape[0]
    features = vision.shape[1]
    near_id = my_near.reshape(1).astype(jnp.int32)

    own_text = jnp.stack(
        (text_queries.reshape(lines, HEAD_WIDTH), text_grads.reshape(lines, HEAD_WIDTH))
    )
    own_text = jnp.broadcast_to(own_text[None], (far, *own_text.shape))
    own_text, vision_keys, video_value_rows = lax.optimization_barrier(
        (own_text, vision_keys, video_value_rows)
    )
    text = lax.all_to_all(own_text, FAR, 0, 0, tiled=True)
    own_kv = jnp.stack((vision_keys, video_value_rows))
    all_kv = from_ring([own_kv] * near, NEAR)
    all_text = from_ring([text] * near, NEAR)

    line_ids = jnp.arange(far * lines, dtype=jnp.int32)
    sources = jnp.stack(bases_from(my_near, near))
    row_of = (
        (line_ids // lines)[None, :] * (near * own_rows)
        + sources[:, None] * own_rows
        + (line_ids % lines // members)[None, :]
    )
    begin, end = row_bounds(lengths, frame_range, row_of.reshape(-1))
    steps = jnp.arange(FRAME_DEV, dtype=jnp.int32)
    first = (my_far * near + sources) * FRAME_DEV
    group_frames = (first[:, None] + steps[None, :]).reshape(-1)
    own_off = offsets(begin[: far * lines], end[: far * lines], group_frames)
    all_off = offsets(begin, end, first[0] + steps)
    chunks = far * lines // CHUNK
    all_off = all_off.reshape(near, chunks, FRAME_DEV, CHUNK)

    part = features // peers
    turned = pl.pallas_call(
        turn_kernel,
        out_shape=jax.ShapeDtypeStruct((near, far, part, kv_rows), BF16),
        grid=(far // 4,),
        in_specs=[SCALARS, pl.BlockSpec((kv_rows, 4 * near * part), lambda i: (0, i))],
        out_specs=pl.BlockSpec((near, 4, part, kv_rows), lambda i: (0, i, 0, 0)),
        compiler_params=LARGER,
    )(near_id, vision)
    turned = turned.reshape(near, far * part, kv_rows)
    text, turned = lax.optimization_barrier((text, turned))

    stats = pl.pallas_call(
        stats_kernel,
        out_shape=jax.ShapeDtypeStruct((far, 3 * chunks, CHUNK), F32),
        in_specs=[WHOLE] * (2 + near),
        out_specs=WHOLE,
        scratch_shapes=[pltpu.VMEM((3 * chunks, CHUNK), F32)],
        compiler_params=PARAMS,
    )(text, own_off, *all_kv)
    stats = lax.all_to_all(stats, FAR, 0, 0, tiled=True)
    norms = pl.pallas_call(
        join_kernel,
        out_shape=jax.ShapeDtypeStruct((near, 2 * chunks, CHUNK), F32),
        in_specs=[WHOLE],
        out_specs=WHOLE,
        compiler_params=PARAMS,
    )(stats)
    all_norm = lax.all_to_all(norms, NEAR, 0, 0, tiled=True)

    dq = pl.pallas_call(
        query_kernel,
        out_shape=jax.ShapeDtypeStruct((far, lines, HEAD_WIDTH), F32),
        in_specs=[WHOLE] * (3 + near),
        out_specs=WHOLE,
        scratch_shapes=[pltpu.VMEM((kv_rows, CHUNK), BF16)],
        compiler_params=PARAMS,
    )(text, own_off, norms, *all_kv)
    dq, all_norm = lax.optimization_barrier((dq, all_norm))
    dq = lax.all_to_all(dq, FAR, 0, 0, tiled=True)

    sums = pl.pallas_call(
        token_kernel,
        out_shape=[jax.ShapeDtypeStruct((kv_rows, 2 * HEAD_WIDTH), BF16)]
        + [jax.ShapeDtypeStruct((far * part, 2 * HEAD_WIDTH), BF16)] * (near - 1),
        in_specs=[SCALARS] + [WHOLE] * 3 + [pl.BlockSpec(memory_space=pltpu.HBM)] + [WHOLE] * near,
        out_specs=[WHOLE] * near,
        scratch_shapes=[
            pltpu.VMEM((kv_rows, CHUNK), BF16),
            pltpu.VMEM((kv_rows, CHUNK), BF16),
            pltpu.VMEM((kv_rows, 2 * HEAD_WIDTH), BF16),
            pltpu.VMEM((near, far * part, kv_rows), BF16),
            pltpu.SemaphoreType.DMA((near,)),
        ],
        compiler_params=LARGE,
        cost_estimate=HEAVY,
    )(near_id, own_kv, all_off, all_norm, turned, *all_text)

    got = from_ring(sums, NEAR)
    got[0] = pl.pallas_call(
        own_kernel,
        out_shape=jax.ShapeDtypeStruct((far * part, 2 * HEAD_WIDTH), BF16),
        grid=(1,),
        in_specs=[
            pl.BlockSpec((1, far * part, kv_rows), lambda i: (0, 0, 0)),
            pl.BlockSpec((kv_rows, 2 * HEAD_WIDTH), lambda i: (0, 0)),
        ],
        out_specs=pl.BlockSpec((far * part, 2 * HEAD_WIDTH), lambda i: (0, 0)),
        compiler_params=LARGE,
    )(turned, sums[0])

    dq = pl.pallas_call(
        sum_kernel,
        out_shape=jax.ShapeDtypeStruct((lines, HEAD_WIDTH), BF16),
        in_specs=[WHOLE],
        out_specs=WHOLE,
        compiler_params=PARAMS,
        cost_estimate=HEAVY,
    )(dq)
    dq = from_everyone(dq.reshape(own_rows, -1), FAR).reshape(far, own_rows, -1)

    weights = sum(one.astype(F32) for one in got).astype(BF16)
    weights, dq = lax.optimization_barrier((weights, dq))
    weights = lax.all_to_all(
        weights.reshape(far, part, 2 * HEAD_WIDTH), FAR, 0, 0, tiled=True
    )
    all_dq = from_ring([dq] * near, NEAR)
    query_grad = jnp.stack([lax.select_n(base, *all_dq) for base in bases_from(my_near, near)], 1)
    query_grad = query_grad.reshape(peers * own_rows, -1)
    key_weights, value_weights = pl.pallas_call(
        total_kernel,
        out_shape=[jax.ShapeDtypeStruct((part, HEAD_WIDTH), F32)] * 2,
        in_specs=[WHOLE],
        out_specs=[WHOLE] * 2,
        compiler_params=PARAMS,
    )(weights)
    return query_grad, key_weights, value_weights


def solution(mesh):
    finer = Mesh(
        mesh.devices.reshape(2, 8, 4, mesh.shape["head"]), ("tok_0", "tok_1", "tok_2", "head")
    )
    return jax.shard_map(
        shards,
        mesh=finer,
        in_specs=(
            P(TOK, "head"),
            P(TOK, "head"),
            P(TOK, "head"),
            P(TOK, "head"),
            P(TOK, None),
            P(),
            P(),
        ),
        out_specs=(P(None, "head"), P(TOK, "head"), P(TOK, "head")),
        check_vma=False,
    )
```
